32 devices in a mesh: vocab: 8 (over z, y), seq: 4 (over x, core).
Axes of the slice: x: 2, y: 2, z: 4, core: 2. Of those that a mesh axis runs over, the one named last changes fastest.
Arguments:
- hidden: bfloat16 [512, 3584], P('seq', 'vocab'), may hold values from -16 to 16, as said below
- weight: bfloat16 [32000, 3584], P(('vocab', 'seq')), may hold values from -1 to 1, as said below
- targets: int32 [512], P('seq'), may hold values from 0 to 31999
- loss_mask: int32 [512], P('seq'), may hold values from 0 to 1, as said below
Outputs:
- lse: float32 [512], P('seq')
- token_loss: float32 [512], P('seq')
- ce_mean: float32 [], replicated
- z_root: float32 [], replicated
The draws below stay inside these ranges and needn't reach their ends.
Inputs may be any that keep to these rules, and one draw needn't show every extreme that they name: Each token's hidden state, of order one. `weight`: rows of order one over the square root of 3584. `loss_mask`: at least one token is counted.
All inputs are finite; a program needn't handle non-finite values.
Results may differ from the reference program's by a relative error of at most 0.0003.
Values may be sent and summed in bfloat16 or wider, within the bound.
A program may use at most 64 MiB of HBM per device.

```python
import math
import jax
import jax.numpy as jnp
from jax import lax

D = 3584
VOC_DEV = 1000
VOCAB = 32000
TOKENS = 512
N_SEQ = 4


def joint_draw(key):
    key_weight, key_hidden = jax.random.split(jax.random.fold_in(key, 7), 2)
    weight = jax.random.normal(key_weight, (VOCAB, D), jnp.float32) * (3.0 / math.sqrt(D))
    weight = jnp.clip(weight, -1.0, 1.0)
    hidden = jnp.clip(jax.random.normal(key_hidden, (TOKENS, D), jnp.float32), -6.0, 6.0)
    return (weight, hidden)


def draw_hidden(key, part):
    return joint_draw(key)[1].astype(jnp.bfloat16)


def draw_weight(key, part):
    return joint_draw(key)[0].astype(jnp.bfloat16)


def draw_loss_mask(key, part):
    key_bits, key_spot = jax.random.split(jax.random.fold_in(key, 11))
    position = jnp.arange(TOKENS, dtype=jnp.int32)
    bits = jax.random.randint(key_bits, (TOKENS,), 0, 1000)
    keep = (bits < 250 + 650 * position // TOKENS).astype(jnp.int32)
    spot = jax.random.randint(key_spot, (), 0, TOKENS)
    return keep.at[spot].set(1)


def set_ends(drawn, key, low, top_value):
    dims = drawn.shape
    spot = [jax.random.randint(jax.random.fold_in(key, axis), (), 0, dims[axis]) for axis in range(len(dims))]
    drawn = drawn.at[tuple(spot)].set(low)
    longest = dims.index(max(dims))
    spot[longest] = (spot[longest] + 1) % dims[longest]
    return drawn.at[tuple(spot)].set(top_value)


def setup_inputs(seed: int = 0) -> dict:
    key_of = jax.random.split(jax.random.key(seed), 5)
    hidden = draw_hidden(jax.random.fold_in(key_of[4], 71), 0)
    weight = draw_weight(jax.random.fold_in(key_of[4], 71), 0)
    targets = set_ends(jax.random.randint(key_of[2], (TOKENS,), 0, VOCAB), jax.random.fold_in(key_of[2], 1), 0, VOCAB - 1).astype(jnp.int32)
    loss_mask = draw_loss_mask(jax.random.fold_in(key_of[4], 71), 0)
    return {"hidden": hidden, "weight": weight, "targets": targets, "loss_mask": loss_mask}


def reference(hidden, weight, targets, loss_mask):
    block = VOC_DEV * N_SEQ
    count_blocks = VOCAB // block
    stacked = weight.reshape(count_blocks, block, D)
    indices = jnp.arange(count_blocks, dtype=jnp.int32)

    def step(carry, item):
        peak_now, total_now, target_now = carry
        weight_block, index = item
        logits = lax.dot_general(hidden, weight_block, (((1,), (1,)), ((), ())), preferred_element_type=jnp.float32)
        peak_next = jnp.maximum(peak_now, lax.optimization_barrier(jnp.max(logits, axis=1)))
        total_next = total_now * jnp.exp(peak_now - peak_next) + lax.optimization_barrier(jnp.sum(jnp.exp(logits - peak_next[:, None]), axis=1))
        columns = index * block + jnp.arange(block, dtype=jnp.int32)
        target_hit = columns[None, :] == targets[:, None]
        target_next = target_now + lax.optimization_barrier(jnp.sum(jnp.where(target_hit, logits, jnp.float32(0.0)), axis=1))
        return ((peak_next, total_next, target_next), None)
    start = (jnp.full((TOKENS,), -jnp.inf, jnp.float32), jnp.zeros((TOKENS,), jnp.float32), jnp.zeros((TOKENS,), jnp.float32))
    (row_peak, exp_total, target_logit), unused = lax.scan(step, start, (stacked, indices))
    lse = row_peak + jnp.log(exp_total)
    keep = loss_mask.astype(jnp.float32)
    token_loss = keep * (lse - target_logit)
    count = jnp.sum(loss_mask).astype(jnp.float32)
    ce_mean = jnp.sum(token_loss) / count
    z_root = jnp.sqrt(jnp.sum(keep * lse * lse) / count)
    return (lse, token_loss, ce_mean, z_root)
```

```python
import functools
import jax
import jax.numpy as jnp
from jax import lax
from jax.experimental import pallas as pl
from jax.experimental.pallas import tpu as pltpu
from jax.sharding import PartitionSpec as P

MESH = pl.DeviceIdType.MESH
LANES = 128


def general(hidden, weight, targets, loss_mask):
    voc_local = weight.shape[0]
    all_ids = lax.all_gather(targets, "seq", axis=0, tiled=True)
    hidden = lax.all_gather(hidden, "vocab", axis=1, tiled=True)
    logits = lax.dot_general(
        lax.all_gather(hidden, "seq", axis=0, tiled=True),
        weight,
        (((1,), (1,)), ((), ())),
        preferred_element_type=jnp.float32,
    )
    block_index = lax.axis_index("vocab") * lax.axis_size("seq") + lax.axis_index("seq")
    columns = block_index * voc_local + jnp.arange(voc_local, dtype=jnp.int32)
    target_hit = columns[None, :] == all_ids[:, None]
    target_part = jnp.sum(jnp.where(target_hit, logits, jnp.float32(0.0)), axis=1)
    row_peak = lax.pmax(jnp.max(logits, axis=1), ("vocab", "seq"))
    exp_part = jnp.sum(jnp.exp(logits - row_peak[:, None]), axis=1)
    share_exp, share_target = (
        lax.psum_scatter(exp_part, "seq", scatter_dimension=0, tiled=True),
        lax.psum_scatter(target_part, "seq", scatter_dimension=0, tiled=True),
    )
    exp_total, target_logit = lax.psum((share_exp, share_target), "vocab")
    tok_local = targets.shape[0]
    own_peak = lax.dynamic_slice_in_dim(row_peak, lax.axis_index("seq") * tok_local, tok_local, 0)
    lse = own_peak + jnp.log(exp_total)
    keep = loss_mask.astype(jnp.float32)
    token_loss = keep * (lse - target_logit)
    loss_sum, square_sum, count = lax.psum(
        (jnp.sum(token_loss), jnp.sum(keep * lse * lse), jnp.sum(keep)), "seq"
    )
    return (lse, token_loss, loss_sum / count, jnp.sqrt(square_sum / count))


def kernel(
    n_voc, n_seq,
    h_ref, w_hbm, tgt_ref, msk_ref,
    lse_ref, tl_ref, ce_ref, zr_ref,
    G, W, acc, meta, part,
    w_sem, recv, up_sem, down_sem, p_sem, q_sem, sib_sem, meta_send, meta_recv, part_send, part_recv,
):
    Z = n_voc // 2
    n_dev = n_voc * n_seq
    v, s = lax.axis_index("vocab"), lax.axis_index("seq")
    z, y, x, c = v // 2, v % 2, s // 2, s % 2
    me = v * n_seq + s
    voc, toks = w_hbm.shape[0], h_ref.shape[0]
    feat = h_ref.shape[1]
    full = feat // LANES
    half = toks // 2

    load = pltpu.make_async_copy(w_hbm, W, w_sem)
    load.start()

    barrier = pltpu.get_barrier_semaphore()

    def greet(i, carry):
        d = lax.rem(me + i, n_dev)
        pl.semaphore_signal(barrier, inc=1, device_id=(d // n_seq, d % n_seq), device_id_type=MESH)
        return carry

    lax.fori_loop(1, n_dev, greet, 0)

    @pl.when(y == 0)
    def _():
        for j in range(full):
            G[me, j * toks:(j + 1) * toks, :] = h_ref[:, j * LANES:(j + 1) * LANES]
        odd = h_ref[:, full * LANES:feat]
        G[me, full * toks:full * toks + half, :] = jnp.concatenate([odd[:half], odd[half:]], axis=1)

    @pl.when(y == 1)
    def _():
        lead = feat - full * LANES
        for j in range(full):
            G[me, j * toks:(j + 1) * toks, :] = h_ref[:, lead + j * LANES:lead + (j + 1) * LANES]
        odd = h_ref[:, :lead]
        G[me, full * toks:full * toks + half, :] = jnp.concatenate([odd[half:], odd[:half]], axis=1)

    meta[s, 0:1, :] = tgt_ref[...]
    meta[s, 1:2, :] = msk_ref[...]

    pl.semaphore_wait(barrier, n_dev - 1)

    flip_y, flip_x = 1 - 2 * y, 2 - 4 * x
    sib = s + 1 - 2 * c
    p_v, p_s = v + (1 - c) * flip_y, s + c * flip_x
    q_v, q_s = v + c * flip_y, s + (1 - c) * flip_x

    def block(zz, yy, ss):
        return (2 * zz + yy) * n_seq + ss

    def push(b, sem, dv, ds):
        pltpu.make_async_remote_copy(
            src_ref=G.at[b], dst_ref=G.at[b], send_sem=sem, recv_sem=recv.at[b],
            device_id=(dv, ds), device_id_type=MESH,
        ).start()

    def arrived(b):
        pltpu.make_async_remote_copy(
            src_ref=G.at[b], dst_ref=G.at[b], send_sem=sib_sem, recv_sem=recv.at[b],
            device_id=(v, sib), device_id_type=MESH,
        ).wait_recv()

    near = jnp.minimum(z, Z - 1 - z)
    far_side = jnp.where(2 * z < Z, 1, -1)

    def order(i):
        in_near = i <= 2 * near
        sgn = jnp.where(in_near, jnp.where(i % 2 == 1, -1, 1), far_side)
        dist = jnp.where(in_near, (i + 1) // 2, i - near)
        return z + sgn * dist

    def to_sib(b):
        push(b, sib_sem, v, sib)

    def line(zz):
        b = block(zz, y, s)

        @pl.when(jnp.logical_and(zz <= z, z + 1 < Z))
        def _():
            push(b, up_sem.at[zz], v + 2, s)

        @pl.when(jnp.logical_and(zz >= z, z > 0))
        def _():
            push(b, down_sem.at[zz], v - 2, s)

        push(b, p_sem, p_v, p_s)
        push(b, q_sem, q_v, q_s)
        to_sib(b)

    line(z)

    def tell(i, carry):
        d = lax.rem(s + i, n_seq)
        pltpu.make_async_remote_copy(
            src_ref=meta.at[s], dst_ref=meta.at[s], send_sem=meta_send, recv_sem=meta_recv,
            device_id=(v, d), device_id_type=MESH,
        ).start()
        return carry

    lax.fori_loop(1, n_seq, tell, 0)

    p_y, q_y = p_v % 2, q_v % 2

    def from_p(zz):
        b = block(zz, p_y, p_s)
        arrived(b)
        to_sib(b)

    def from_q(zz):
        b = block(zz, q_y, q_s)
        arrived(b)
        to_sib(b)

    def phase1(i, carry):
        zz = order(i)
        arrived(block(zz, y, s))
        line(zz)
        from_p(order(i - 1))

        @pl.when(i >= 2)
        def _():
            from_q(order(i - 2))

        return carry

    lax.fori_loop(1, Z, phase1, 0)

    def on_to_q(zz):
        push(block(zz, p_y, p_s), q_sem, q_v, q_s)

    def early_q(i, carry):
        on_to_q(order(i))
        return carry

    lax.fori_loop(0, Z - 1, early_q, 0)
    from_p(order(Z - 1))
    on_to_q(order(Z - 1))

    def late_q(i, carry):
        from_q(order(i))
        return carry

    lax.fori_loop(max(Z - 2, 0), Z, late_q, 0)

    low = lax.broadcasted_iota(jnp.int32, (half, LANES), 1) < LANES // 2

    def chunk(zz, xx, first):
        sides = []
        for cc in range(2):
            b0, b1 = block(zz, 0, 2 * xx + cc), block(zz, 1, 2 * xx + cc)
            o0 = G[b0, full * toks:full * toks + half, :]
            o1 = G[b1, full * toks:full * toks + half, :]
            top = jnp.where(low, o0, o1)
            turned = jnp.where(low, o1, o0)
            bottom = jnp.concatenate([turned[:, LANES // 2:], turned[:, :LANES // 2]], axis=1)
            tiles = [G[b0, j * toks:(j + 1) * toks, :] for j in range(full)]
            tiles.append(jnp.concatenate([top, bottom], axis=0))
            tiles += [G[b1, j * toks:(j + 1) * toks, :] for j in range(full)]
            sides.append(jnp.concatenate(tiles, axis=1))
        rows = jnp.concatenate(sides, axis=0)
        cols = pl.ds(pl.multiple_of(zz * 2 * feat, LANES), 2 * feat)
        out = lax.dot_general(
            W[:, cols], rows, (((1,), (1,)), ((), ())), preferred_element_type=jnp.float32
        )

        @pl.when(first)
        def _():
            acc[xx] = out

        @pl.when(jnp.logical_not(first))
        def _():
            acc[xx] += out

    step = max(r for r in range(8, 257, 8) if voc % r == 0)

    def finish(xx):
        ids = jnp.concatenate([meta[2 * xx, 0:1, :], meta[2 * xx + 1, 0:1, :]], axis=1)
        ids = ids - me * voc
        wide = (8, 2 * toks)

        def peak(r, m):
            tile = acc[xx, pl.ds(pl.multiple_of(r * step, 8), step), :]
            return jnp.maximum(m, jnp.max(tile.reshape(step // 8, 8, 2 * toks), axis=0))

        m = lax.fori_loop(0, voc // step, peak, jnp.full(wide, -jnp.inf, jnp.float32))
        m = jnp.max(m, axis=0, keepdims=True)

        def total(r, carry):
            e, t = carry
            tile = acc[xx, pl.ds(pl.multiple_of(r * step, 8), step), :]
            row = lax.broadcasted_iota(jnp.int32, (step, 2 * toks), 0) + r * step
            hit = jnp.where(row == ids, tile, jnp.float32(0.0))
            e += jnp.sum(jnp.exp(tile - m).reshape(step // 8, 8, 2 * toks), axis=0)
            t += jnp.sum(hit.reshape(step // 8, 8, 2 * toks), axis=0)
            return e, t

        zero = jnp.zeros(wide, jnp.float32)
        e, t = lax.fori_loop(0, voc // step, total, (zero, zero))
        lse = m + jnp.log(jnp.sum(e, axis=0, keepdims=True))
        t = jnp.sum(t, axis=0, keepdims=True)
        for cc in range(2):
            cut = slice(cc * toks, (cc + 1) * toks)
            part[me, pl.ds(2 * xx + cc, 1), :] = lse[:, cut]
            part[me, pl.ds(n_seq + 2 * xx + cc, 1), :] = t[:, cut]

    load.wait()

    def near_chunk(i, carry):
        zz = order(i)
        arrived(block(zz, y, sib))
        arrived(block(zz, 1 - y, sib))
        chunk(zz, x, i == 0)
        return carry

    lax.fori_loop(0, Z, near_chunk, 0)

    pltpu.make_async_copy(meta.at[0:n_seq - 1], meta.at[0:n_seq - 1], meta_recv).wait()

    def far_chunk(i, carry):
        zz = order(i)
        b = block(zz, 1 - y, s + flip_x)
        arrived(b)
        to_sib(b)

        @pl.when(i == 0)
        def _():
            finish(x)

        arrived(block(zz, y, sib + flip_x))
        arrived(block(zz, 1 - y, sib + flip_x))
        chunk(zz, 1 - x, i == 0)
        return carry

    lax.fori_loop(0, Z, far_chunk, 0)
    finish(1 - x)

    def share(i, carry):
        d = lax.rem(me + i, n_dev)
        pltpu.make_async_remote_copy(
            src_ref=part.at[me], dst_ref=part.at[me], send_sem=part_send, recv_sem=part_recv,
            device_id=(d // n_seq, d % n_seq), device_id_type=MESH,
        ).start()
        return carry

    lax.fori_loop(1, n_dev, share, 0)

    def drain(zz, carry):
        @pl.when(jnp.logical_and(zz <= z, z + 1 < Z))
        def _():
            pltpu.make_async_copy(G.at[0], G.at[0], up_sem.at[zz]).wait()

        @pl.when(jnp.logical_and(zz >= z, z > 0))
        def _():
            pltpu.make_async_copy(G.at[0], G.at[0], down_sem.at[zz]).wait()

        return carry

    lax.fori_loop(0, Z, drain, 0)
    for sem, count in ((p_sem, Z), (q_sem, 2 * Z), (sib_sem, 4 * Z)):
        pltpu.make_async_copy(G.at[0:count], G.at[0:count], sem).wait()
    pltpu.make_async_copy(meta.at[0:n_seq - 1], meta.at[0:n_seq - 1], meta_send).wait()
    pltpu.make_async_copy(part.at[0:n_dev - 1], part.at[0:n_dev - 1], part_recv).wait()

    parts = part[...]
    lses, t = parts[:, :n_seq, :], jnp.sum(parts[:, n_seq:2 * n_seq, :], axis=0)
    top = jnp.max(lses, axis=0)
    lse = top + jnp.log(jnp.sum(jnp.exp(lses - top[None]), axis=0))
    keep = jnp.concatenate([meta[i, 1:2, :] for i in range(n_seq)], axis=0).astype(jnp.float32)
    loss = keep * (lse - t)

    def whole(a):
        return jnp.sum(jnp.sum(a, axis=0, keepdims=True), axis=1, keepdims=True)

    count = whole(keep)
    ce_ref[...] = whole(loss) / count
    zr_ref[...] = jnp.sqrt(whole(keep * lse * lse) / count)
    mine = lax.broadcasted_iota(jnp.int32, (n_seq, toks), 0) == s
    lse_ref[...] = jnp.sum(jnp.where(mine, lse, 0.0), axis=0, keepdims=True)
    tl_ref[...] = jnp.sum(jnp.where(mine, loss, 0.0), axis=0, keepdims=True)
    pltpu.make_async_copy(part.at[0:n_dev - 1], part.at[0:n_dev - 1], part_send).wait()


def on_device(n_voc, n_seq, hidden, weight, targets, loss_mask):
    toks, feat = hidden.shape
    voc, wide = weight.shape
    fits = (
        n_seq == 4 and n_voc % 2 == 0 and toks == LANES
        and feat % LANES == LANES // 2 and voc % 8 == 0
    )
    if not fits:
        return general(hidden, weight, targets, loss_mask)
    n_dev = n_voc * n_seq
    n_z = n_voc // 2
    f32 = jnp.float32
    dma = pltpu.SemaphoreType.DMA
    vmem = pl.BlockSpec(memory_space=pltpu.VMEM)
    lse, loss, ce, root = pl.pallas_call(
        functools.partial(kernel, n_voc, n_seq),
        out_shape=(
            jax.ShapeDtypeStruct((1, toks), f32),
            jax.ShapeDtypeStruct((1, toks), f32),
            jax.ShapeDtypeStruct((1, 1), f32),
            jax.ShapeDtypeStruct((1, 1), f32),
        ),
        in_specs=[vmem, pl.BlockSpec(memory_space=pl.ANY), vmem, vmem],
        out_specs=(vmem, vmem, vmem, vmem),
        scratch_shapes=[
            pltpu.VMEM((n_dev, toks * feat // LANES, LANES), jnp.bfloat16),
            pltpu.VMEM((voc, wide), jnp.bfloat16),
            pltpu.VMEM((2, voc, 2 * toks), f32),
            pltpu.VMEM((n_seq, 8, LANES), jnp.int32),
            pltpu.VMEM((n_dev, 2 * n_seq, LANES), f32),
            dma, dma((n_dev,)), dma((n_z,)), dma((n_z,)),
            dma, dma, dma, dma, dma, dma, dma,
        ],
        compiler_params=pltpu.CompilerParams(
            collective_id=0, has_side_effects=True, vmem_limit_bytes=48 * 2**20
        ),
        cost_estimate=pl.CostEstimate(
            flops=2 * n_seq * toks * wide * voc, bytes_accessed=2 * voc * wide,
            transcendentals=n_seq * toks * voc,
        ),
    )(hidden, weight, targets.reshape(1, toks), loss_mask.reshape(1, toks))
    return (lse.reshape(toks), loss.reshape(toks), ce.reshape(()), root.reshape(()))


def solution(mesh):
    in_specs = (P("seq", "vocab"), P(("vocab", "seq"), None), P("seq"), P("seq"))
    out_specs = (P("seq"), P("seq"), P(), P())
    return jax.shard_map(
        functools.partial(on_device, mesh.shape["vocab"], mesh.shape["seq"]),
        mesh=mesh, in_specs=in_specs, out_specs=out_specs, check_vma=False,
    )
```

```python
import functools
import jax
import jax.numpy as jnp
from jax import lax
from jax.experimental import pallas as pl
from jax.experimental.pallas import tpu as pltpu
from jax.sharding import PartitionSpec as P

MESH = pl.DeviceIdType.MESH
LANES = 128


def general(hidden, weight, targets, loss_mask):
    voc_local = weight.shape[0]
    all_ids = lax.all_gather(targets, "seq", axis=0, tiled=True)
    hidden = lax.all_gather(hidden, "vocab", axis=1, tiled=True)
    logits = lax.dot_general(
        lax.all_gather(hidden, "seq", axis=0, tiled=True),
        weight,
        (((1,), (1,)), ((), ())),
        preferred_element_type=jnp.float32,
    )
    block_index = lax.axis_index("vocab") * lax.axis_size("seq") + lax.axis_index("seq")
    columns = block_index * voc_local + jnp.arange(voc_local, dtype=jnp.int32)
    target_hit = columns[None, :] == all_ids[:, None]
    target_part = jnp.sum(jnp.where(target_hit, logits, jnp.float32(0.0)), axis=1)
    row_peak = lax.pmax(jnp.max(logits, axis=1), ("vocab", "seq"))
    exp_part = jnp.sum(jnp.exp(logits - row_peak[:, None]), axis=1)
    share_exp, share_target = (
        lax.psum_scatter(exp_part, "seq", scatter_dimension=0, tiled=True),
        lax.psum_scatter(target_part, "seq", scatter_dimension=0, tiled=True),
    )
    exp_total, target_logit = lax.psum((share_exp, share_target), "vocab")
    tok_local = targets.shape[0]
    own_peak = lax.dynamic_slice_in_dim(row_peak, lax.axis_index("seq") * tok_local, tok_local, 0)
    lse = own_peak + jnp.log(exp_total)
    keep = loss_mask.astype(jnp.float32)
    token_loss = keep * (lse - target_logit)
    loss_sum, square_sum, count = lax.psum(
        (jnp.sum(token_loss), jnp.sum(keep * lse * lse), jnp.sum(keep)), "seq"
    )
    return (lse, token_loss, loss_sum / count, jnp.sqrt(square_sum / count))


def kernel(
    n_voc, n_seq,
    h_ref, w_hbm, tgt_ref, msk_ref,
    lse_ref, tl_ref, ce_ref, zr_ref,
    G, W, acc, meta, part, done,
    w_sem, in_sem, recv, up_sem, down_sem, p_sem, q_sem, sib_sem, meta_send, meta_recv, part_send, part_recv,
):
    Z = n_voc // 2
    n_dev = n_voc * n_seq
    v, s = lax.axis_index("vocab"), lax.axis_index("seq")
    z, y, x, c = v // 2, v % 2, s // 2, s % 2
    me = v * n_seq + s
    voc = w_hbm.shape[0]
    feat, toks = h_ref.shape

    own = (
        pltpu.make_async_copy(h_ref, G.at[me], in_sem.at[0]),
        pltpu.make_async_copy(tgt_ref, meta.at[s, pl.ds(0, 1)], in_sem.at[1]),
        pltpu.make_async_copy(msk_ref, meta.at[s, pl.ds(1, 1)], in_sem.at[2]),
    )
    for copy in own:
        copy.start()
    load = pltpu.make_async_copy(w_hbm, W, w_sem)
    load.start()

    barrier = pltpu.get_barrier_semaphore()

    def greet(i, carry):
        d = lax.rem(me + i, n_dev)
        pl.semaphore_signal(barrier, inc=1, device_id=(d // n_seq, d % n_seq), device_id_type=MESH)
        return carry

    lax.fori_loop(1, n_dev, greet, 0)

    for copy in own:
        copy.wait()
    pl.semaphore_wait(barrier, n_dev - 1)

    flip_y, flip_x = 1 - 2 * y, 2 - 4 * x
    sib = s + 1 - 2 * c
    p_v, p_s = v + (1 - c) * flip_y, s + c * flip_x
    q_v, q_s = v + c * flip_y, s + (1 - c) * flip_x

    def block(zz, yy, ss):
        return (2 * zz + yy) * n_seq + ss

    def push(b, sem, dv, ds):
        pltpu.make_async_remote_copy(
            src_ref=G.at[b], dst_ref=G.at[b], send_sem=sem, recv_sem=recv.at[b],
            device_id=(dv, ds), device_id_type=MESH,
        ).start()

    def arrived(b):
        pltpu.make_async_remote_copy(
            src_ref=G.at[b], dst_ref=G.at[b], send_sem=sib_sem, recv_sem=recv.at[b],
            device_id=(v, sib), device_id_type=MESH,
        ).wait_recv()

    near = jnp.minimum(z, Z - 1 - z)
    far_side = jnp.where(2 * z < Z, 1, -1)

    def order(i):
        in_near = i <= 2 * near
        sgn = jnp.where(in_near, jnp.where(i % 2 == 1, -1, 1), far_side)
        dist = jnp.where(in_near, (i + 1) // 2, i - near)
        return z + sgn * dist

    def to_sib(b):
        push(b, sib_sem, v, sib)

    def line(zz):
        b = block(zz, y, s)

        @pl.when(jnp.logical_and(zz <= z, z + 1 < Z))
        def _():
            push(b, up_sem.at[zz], v + 2, s)

        @pl.when(jnp.logical_and(zz >= z, z > 0))
        def _():
            push(b, down_sem.at[zz], v - 2, s)

        push(b, p_sem, p_v, p_s)
        push(b, q_sem, q_v, q_s)
        to_sib(b)

    line(z)

    def tell(i, carry):
        d = lax.rem(s + i, n_seq)
        pltpu.make_async_remote_copy(
            src_ref=meta.at[s], dst_ref=meta.at[s], send_sem=meta_send, recv_sem=meta_recv,
            device_id=(v, d), device_id_type=MESH,
        ).start()
        return carry

    lax.fori_loop(1, n_seq, tell, 0)

    p_y, q_y = p_v % 2, q_v % 2

    def from_p(zz):
        b = block(zz, p_y, p_s)
        arrived(b)
        to_sib(b)

    def from_q(zz):
        b = block(zz, q_y, q_s)
        arrived(b)
        to_sib(b)

    def chunk(zz, xx, first):
        sides = []
        for cc in range(2):
            pair = [G[block(zz, yy, 2 * xx + cc)] for yy in range(2)]
            sides.append(jnp.concatenate(pair, axis=0))
        rows = jnp.concatenate(sides, axis=1)
        cols = pl.ds(pl.multiple_of(zz * 2 * feat, LANES), 2 * feat)
        out = lax.dot_general(
            W[:, cols], rows, (((1,), (0,)), ((), ())), preferred_element_type=jnp.float32
        )

        @pl.when(first)
        def _():
            acc[xx] = out

        @pl.when(jnp.logical_not(first))
        def _():
            acc[xx] += out

    step = max(r for r in range(8, 257, 8) if voc % r == 0)

    def finish(xx):
        ids = jnp.concatenate([meta[2 * xx, 0:1, :], meta[2 * xx + 1, 0:1, :]], axis=1)
        ids = ids - me * voc
        wide = (8, 2 * toks)

        def peak(r, m):
            tile = acc[xx, pl.ds(pl.multiple_of(r * step, 8), step), :]
            return jnp.maximum(m, jnp.max(tile.reshape(step // 8, 8, 2 * toks), axis=0))

        m = lax.fori_loop(0, voc // step, peak, jnp.full(wide, -jnp.inf, jnp.float32))
        m = jnp.max(m, axis=0, keepdims=True)

        def total(r, carry):
            e, t = carry
            tile = acc[xx, pl.ds(pl.multiple_of(r * step, 8), step), :]
            row = lax.broadcasted_iota(jnp.int32, (step, 2 * toks), 0) + r * step
            hit = jnp.where(row == ids, tile, jnp.float32(0.0))
            e += jnp.sum(jnp.exp(tile - m).reshape(step // 8, 8, 2 * toks), axis=0)
            t += jnp.sum(hit.reshape(step // 8, 8, 2 * toks), axis=0)
            return e, t

        zero = jnp.zeros(wide, jnp.float32)
        e, t = lax.fori_loop(0, voc // step, total, (zero, zero))
        lse = m + jnp.log(jnp.sum(e, axis=0, keepdims=True))
        t = jnp.sum(t, axis=0, keepdims=True)
        for cc in range(2):
            cut = slice(cc * toks, (cc + 1) * toks)
            part[me, pl.ds(2 * xx + cc, 1), :] = lse[:, cut]
            part[me, pl.ds(n_seq + 2 * xx + cc, 1), :] = t[:, cut]

    def do_chunk(k):
        zz, far = order(k % Z), k // Z
        xx = x + far * (1 - 2 * x)
        ss = 2 * xx + 1 - c
        arrived(block(zz, 0, ss))
        arrived(block(zz, 1, ss))
        chunk(zz, xx, k % Z == 0)

    def phase1(i, carry):
        zz = order(i)
        arrived(block(zz, y, s))
        line(zz)
        from_p(order(i - 1))

        @pl.when(i >= 2)
        def _():
            from_q(order(i - 2))

        @pl.when(i == 3)
        def _():
            load.wait()

        @pl.when(i >= 3)
        def _():
            do_chunk(i - 3)

        return carry

    lax.fori_loop(1, Z, phase1, 0)

    def on_to_q(zz):
        push(block(zz, p_y, p_s), q_sem, q_v, q_s)

    def early_q(i, carry):
        on_to_q(order(i))
        return carry

    lax.fori_loop(0, Z - 1, early_q, 0)
    from_p(order(Z - 1))
    on_to_q(order(Z - 1))

    def late_q(i, carry):
        from_q(order(i))
        do_chunk(i - 1)
        return carry

    lax.fori_loop(Z - 2, Z, late_q, 0)
    pltpu.make_async_copy(meta.at[0:n_seq - 1], meta.at[0:n_seq - 1], meta_recv).wait()

    def last(i, carry):
        b = block(order(i), 1 - y, s + flip_x)
        arrived(b)
        to_sib(b)
        do_chunk(Z - 1 + i)
        return carry

    lax.fori_loop(0, Z, last, 0)
    finish(x)
    do_chunk(2 * Z - 1)
    finish(1 - x)

    def share(i, carry):
        d = lax.rem(me + i, n_dev)
        pltpu.make_async_remote_copy(
            src_ref=part.at[me], dst_ref=part.at[me], send_sem=part_send, recv_sem=part_recv,
            device_id=(d // n_seq, d % n_seq), device_id_type=MESH,
        ).start()
        return carry

    lax.fori_loop(1, n_dev, share, 0)

    def drain(zz, carry):
        @pl.when(jnp.logical_and(zz <= z, z + 1 < Z))
        def _():
            pltpu.make_async_copy(G.at[0], G.at[0], up_sem.at[zz]).wait()

        @pl.when(jnp.logical_and(zz >= z, z > 0))
        def _():
            pltpu.make_async_copy(G.at[0], G.at[0], down_sem.at[zz]).wait()

        return carry

    lax.fori_loop(0, Z, drain, 0)
    for sem, count in ((p_sem, Z), (q_sem, 2 * Z), (sib_sem, 4 * Z)):
        pltpu.make_async_copy(G.at[0:count], G.at[0:count], sem).wait()
    pltpu.make_async_copy(meta.at[0:n_seq - 1], meta.at[0:n_seq - 1], meta_send).wait()
    pltpu.make_async_copy(part.at[0:n_dev - 1], part.at[0:n_dev - 1], part_recv).wait()

    parts = part[...]
    lses, t = parts[:, :n_seq, :], jnp.sum(parts[:, n_seq:2 * n_seq, :], axis=0)
    top = jnp.max(lses, axis=0)
    lse = top + jnp.log(jnp.sum(jnp.exp(lses - top[None]), axis=0))
    keep = jnp.concatenate([meta[i, 1:2, :] for i in range(n_seq)], axis=0).astype(jnp.float32)
    loss = keep * (lse - t)

    def whole(a):
        return jnp.sum(jnp.sum(a, axis=0, keepdims=True), axis=1, keepdims=True)

    count = whole(keep)
    ce_ref[...] = whole(loss) / count
    zr_ref[...] = jnp.sqrt(whole(keep * lse * lse) / count)
    mine = lax.broadcasted_iota(jnp.int32, (n_seq, toks), 0) == s
    done[0] = jnp.sum(jnp.where(mine, lse, 0.0), axis=0, keepdims=True)
    done[1] = jnp.sum(jnp.where(mine, loss, 0.0), axis=0, keepdims=True)
    out = (
        pltpu.make_async_copy(done.at[0], lse_ref, in_sem.at[0]),
        pltpu.make_async_copy(done.at[1], tl_ref, in_sem.at[1]),
    )
    for copy in out:
        copy.start()
    for copy in out:
        copy.wait()
    pltpu.make_async_copy(part.at[0:n_dev - 1], part.at[0:n_dev - 1], part_send).wait()


def on_device(n_voc, n_seq, hidden, weight, targets, loss_mask):
    toks, feat = hidden.shape
    sub = 16
    voc, wide = weight.shape
    fits = (
        n_seq == 4 and n_voc % 2 == 0 and n_voc >= 8 and toks == LANES
        and feat % sub == 0 and 2 * feat % LANES == 0 and voc % 8 == 0
    )
    if not fits:
        return general(hidden, weight, targets, loss_mask)
    n_dev = n_voc * n_seq
    n_z = n_voc // 2
    f32 = jnp.float32
    dma = pltpu.SemaphoreType.DMA
    vmem = pl.BlockSpec(memory_space=pltpu.VMEM)
    hbm = pl.BlockSpec(memory_space=pltpu.HBM)
    lse, loss, ce, root = pl.pallas_call(
        functools.partial(kernel, n_voc, n_seq),
        out_shape=(
            jax.ShapeDtypeStruct((1, toks), f32),
            jax.ShapeDtypeStruct((1, toks), f32),
            jax.ShapeDtypeStruct((1, 1), f32),
            jax.ShapeDtypeStruct((1, 1), f32),
        ),
        in_specs=[hbm, hbm, hbm, hbm],
        out_specs=(hbm, hbm, vmem, vmem),
        scratch_shapes=[
            pltpu.VMEM((n_dev, feat, toks), jnp.bfloat16),
            pltpu.VMEM((voc, wide), jnp.bfloat16),
            pltpu.VMEM((2, voc, 2 * toks), f32),
            pltpu.VMEM((n_seq, 8, LANES), jnp.int32),
            pltpu.VMEM((n_dev, 2 * n_seq, LANES), f32),
            pltpu.VMEM((2, 1, toks), f32),
            dma, dma((3,)), dma((n_dev,)), dma((n_z,)), dma((n_z,)),
            dma, dma, dma, dma, dma, dma, dma,
        ],
        compiler_params=pltpu.CompilerParams(
            collective_id=0, has_side_effects=True, vmem_limit_bytes=64 * 2**20
        ),
        cost_estimate=pl.CostEstimate(
            flops=2 * n_seq * toks * wide * voc, bytes_accessed=2 * voc * wide,
            transcendentals=n_seq * toks * voc,
        ),
    )(hidden.T, weight, targets.reshape(1, toks), loss_mask.reshape(1, toks))
    return (lse.reshape(toks), loss.reshape(toks), ce.reshape(()), root.reshape(()))


def solution(mesh):
    in_specs = (P("seq", "vocab"), P(("vocab", "seq"), None), P("seq"), P("seq"))
    out_specs = (P("seq"), P("seq"), P(), P())
    return jax.shard_map(
        functools.partial(on_device, mesh.shape["vocab"], mesh.shape["seq"]),
        mesh=mesh, in_specs=in_specs, out_specs=out_specs, check_vma=False,
    )
```

```python
import functools
import jax
import jax.numpy as jnp
from jax import lax
from jax.experimental import pallas as pl
from jax.experimental.pallas import tpu as pltpu
from jax.sharding import PartitionSpec as P

MESH = pl.DeviceIdType.MESH
LANES = 128


def general(hidden, weight, targets, loss_mask):
    voc_local = weight.shape[0]
    all_ids = lax.all_gather(targets, "seq", axis=0, tiled=True)
    hidden = lax.all_gather(hidden, "vocab", axis=1, tiled=True)
    logits = lax.dot_general(
        lax.all_gather(hidden, "seq", axis=0, tiled=True),
        weight,
        (((1,), (1,)), ((), ())),
        preferred_element_type=jnp.float32,
    )
    block_index = lax.axis_index("vocab") * lax.axis_size("seq") + lax.axis_index("seq")
    columns = block_index * voc_local + jnp.arange(voc_local, dtype=jnp.int32)
    target_hit = columns[None, :] == all_ids[:, None]
    target_part = jnp.sum(jnp.where(target_hit, logits, jnp.float32(0.0)), axis=1)
    row_peak = lax.pmax(jnp.max(logits, axis=1), ("vocab", "seq"))
    exp_part = jnp.sum(jnp.exp(logits - row_peak[:, None]), axis=1)
    share_exp, share_target = (
        lax.psum_scatter(exp_part, "seq", scatter_dimension=0, tiled=True),
        lax.psum_scatter(target_part, "seq", scatter_dimension=0, tiled=True),
    )
    exp_total, target_logit = lax.psum((share_exp, share_target), "vocab")
    tok_local = targets.shape[0]
    own_peak = lax.dynamic_slice_in_dim(row_peak, lax.axis_index("seq") * tok_local, tok_local, 0)
    lse = own_peak + jnp.log(exp_total)
    keep = loss_mask.astype(jnp.float32)
    token_loss = keep * (lse - target_logit)
    loss_sum, square_sum, count = lax.psum(
        (jnp.sum(token_loss), jnp.sum(keep * lse * lse), jnp.sum(keep)), "seq"
    )
    return (lse, token_loss, loss_sum / count, jnp.sqrt(square_sum / count))


def kernel(
    n_voc, n_seq,
    h_ref, w_hbm, tgt_ref, msk_ref,
    tok_ref, ce_ref, zr_ref,
    G, W, acc, meta, part, done,
    w_sem, in_sem, recv, up_sem, down_sem, p_sem, q_sem, sib_sem, meta_send, meta_recv, part_send, part_recv,
):
    Z = n_voc // 2
    n_dev = n_voc * n_seq
    v, s = lax.axis_index("vocab"), lax.axis_index("seq")
    z, y, x, c = v // 2, v % 2, s // 2, s % 2
    me = v * n_seq + s
    voc = w_hbm.shape[0]
    feat, toks = h_ref.shape

    own = (
        pltpu.make_async_copy(h_ref, G.at[me], in_sem.at[0]),
        pltpu.make_async_copy(tgt_ref, meta.at[s, pl.ds(0, 1)], in_sem.at[1]),
        pltpu.make_async_copy(msk_ref, meta.at[s, pl.ds(1, 1)], in_sem.at[2]),
    )
    for copy in own:
        copy.start()
    load = pltpu.make_async_copy(w_hbm, W, w_sem)
    load.start()

    barrier = pltpu.get_barrier_semaphore()

    def greet(i, carry):
        d = lax.rem(me + i, n_dev)
        pl.semaphore_signal(barrier, inc=1, device_id=(d // n_seq, d % n_seq), device_id_type=MESH)
        return carry

    lax.fori_loop(1, n_dev, greet, 0)

    for copy in own:
        copy.wait()
    pl.semaphore_wait(barrier, n_dev - 1)

    flip_y, flip_x = 1 - 2 * y, 2 - 4 * x
    sib = s + 1 - 2 * c
    p_v, p_s = v + (1 - c) * flip_y, s + c * flip_x
    q_v, q_s = v + c * flip_y, s + (1 - c) * flip_x

    def block(zz, yy, ss):
        return (2 * zz + yy) * n_seq + ss

    def push(b, sem, dv, ds):
        pltpu.make_async_remote_copy(
            src_ref=G.at[b], dst_ref=G.at[b], send_sem=sem, recv_sem=recv.at[b],
            device_id=(dv, ds), device_id_type=MESH,
        ).start()

    def arrived(b):
        pltpu.make_async_remote_copy(
            src_ref=G.at[b], dst_ref=G.at[b], send_sem=sib_sem, recv_sem=recv.at[b],
            device_id=(v, sib), device_id_type=MESH,
        ).wait_recv()

    near = jnp.minimum(z, Z - 1 - z)
    far_side = jnp.where(2 * z < Z, 1, -1)

    def order(i):
        in_near = i <= 2 * near
        sgn = jnp.where(in_near, jnp.where(i % 2 == 1, -1, 1), far_side)
        dist = jnp.where(in_near, (i + 1) // 2, i - near)
        return z + sgn * dist

    def to_sib(b):
        push(b, sib_sem, v, sib)

    def along(b, zz, side):
        @pl.when(jnp.logical_and(zz <= z, z + 1 < Z))
        def _():
            push(b, up_sem.at[side, zz], v + 2, s)

        @pl.when(jnp.logical_and(zz >= z, z > 0))
        def _():
            push(b, down_sem.at[side, zz], v - 2, s)

    def is_end(zz):
        return jnp.logical_or(zz == 0, zz == Z - 1)

    def line(zz):
        b = block(zz, y, s)
        along(b, zz, 0)

        @pl.when(jnp.logical_or(zz == z, jnp.logical_not(is_end(zz))))
        def _():
            push(b, p_sem.at[zz], p_v, p_s)

        push(b, q_sem, q_v, q_s)
        to_sib(b)

    line(z)

    def tell(i, carry):
        d = lax.rem(s + i, n_seq)
        pltpu.make_async_remote_copy(
            src_ref=meta.at[s], dst_ref=meta.at[s], send_sem=meta_send, recv_sem=meta_recv,
            device_id=(v, d), device_id_type=MESH,
        ).start()
        return carry

    lax.fori_loop(1, n_seq, tell, 0)

    p_y, q_y = p_v % 2, q_v % 2

    def from_p(zz):
        b = block(zz, p_y, p_s)
        arrived(b)

        @pl.when(is_end(zz))
        def _():
            along(b, zz, 1)

        push(b, q_sem, q_v, q_s)
        to_sib(b)

    def from_q(zz, yy, ss):
        b = block(zz, yy, ss)
        arrived(b)
        to_sib(b)

    def chunk(zz, xx, first):
        sides = []
        for cc in range(2):
            pair = [G[block(zz, yy, 2 * xx + cc)] for yy in range(2)]
            sides.append(jnp.concatenate(pair, axis=0))
        rows = jnp.concatenate(sides, axis=1)
        cols = pl.ds(pl.multiple_of(zz * 2 * feat, LANES), 2 * feat)
        out = lax.dot_general(
            W[:, cols], rows, (((1,), (0,)), ((), ())), preferred_element_type=jnp.float32
        )

        @pl.when(first)
        def _():
            acc[xx] = out

        @pl.when(jnp.logical_not(first))
        def _():
            acc[xx] += out

    step = max(r for r in range(8, 257, 8) if voc % r == 0)

    def finish(xx):
        ids = jnp.concatenate([meta[2 * xx, 0:1, :], meta[2 * xx + 1, 0:1, :]], axis=1)
        ids = ids - me * voc
        wide = (8, 2 * toks)

        def peak(r, m):
            tile = acc[xx, pl.ds(pl.multiple_of(r * step, 8), step), :]
            return jnp.maximum(m, jnp.max(tile.reshape(step // 8, 8, 2 * toks), axis=0))

        m = lax.fori_loop(0, voc // step, peak, jnp.full(wide, -jnp.inf, jnp.float32))
        m = jnp.max(m, axis=0, keepdims=True)

        def total(r, carry):
            e, t = carry
            tile = acc[xx, pl.ds(pl.multiple_of(r * step, 8), step), :]
            row = lax.broadcasted_iota(jnp.int32, (step, 2 * toks), 0) + r * step
            hit = jnp.where(row == ids, tile, jnp.float32(0.0))
            e += jnp.sum(jnp.exp(tile - m).reshape(step // 8, 8, 2 * toks), axis=0)
            t += jnp.sum(hit.reshape(step // 8, 8, 2 * toks), axis=0)
            return e, t

        zero = jnp.zeros(wide, jnp.float32)
        e, t = lax.fori_loop(0, voc // step, total, (zero, zero))
        lse = m + jnp.log(jnp.sum(e, axis=0, keepdims=True))
        t = jnp.sum(t, axis=0, keepdims=True)
        for cc in range(2):
            cut = slice(cc * toks, (cc + 1) * toks)
            part[me, pl.ds(2 * xx + cc, 1), :] = lse[:, cut]
            part[me, pl.ds(n_seq + 2 * xx + cc, 1), :] = t[:, cut]

    def do_chunk(k):
        zz, far = order(k % Z), k // Z
        xx = x + far * (1 - 2 * x)
        ss = 2 * xx + 1 - c
        arrived(block(zz, 0, ss))
        arrived(block(zz, 1, ss))
        chunk(zz, xx, k % Z == 0)

    def turn(r, carry):
        @pl.when(r < Z)
        def _():
            zz = order(r)
            arrived(block(zz, y, s))
            line(zz)

        @pl.when(r <= Z)
        def _():
            from_p(order(r - 1))

        @pl.when(jnp.logical_and(r >= 2, r < Z + 2))
        def _():
            from_q(order(r - 2), q_y, q_s)

        @pl.when(r == 3)
        def _():
            load.wait()

        @pl.when(r >= 3)
        def _():
            from_q(order(r - 3), 1 - y, s + flip_x)
            do_chunk(r - 3)

        @pl.when(r >= 4)
        def _():
            do_chunk(Z + r - 4)

        return carry

    lax.fori_loop(1, Z + 3, turn, 0)
    pltpu.make_async_copy(meta.at[0:n_seq - 1], meta.at[0:n_seq - 1], meta_recv).wait()
    finish(x)
    do_chunk(2 * Z - 1)
    finish(1 - x)

    def share(i, carry):
        d = lax.rem(me + i, n_dev)
        pltpu.make_async_remote_copy(
            src_ref=part.at[me], dst_ref=part.at[me], send_sem=part_send, recv_sem=part_recv,
            device_id=(d // n_seq, d % n_seq), device_id_type=MESH,
        ).start()
        return carry

    lax.fori_loop(1, n_dev, share, 0)

    def sent(sem):
        pltpu.make_async_copy(G.at[0], G.at[0], sem).wait()

    def drain(zz, carry):
        for side in range(2):
            also = True if side == 0 else is_end(zz)

            @pl.when(jnp.logical_and(also, jnp.logical_and(zz <= z, z + 1 < Z)))
            def _():
                sent(up_sem.at[side, zz])

            @pl.when(jnp.logical_and(also, jnp.logical_and(zz >= z, z > 0)))
            def _():
                sent(down_sem.at[side, zz])

        @pl.when(jnp.logical_or(zz == z, jnp.logical_not(is_end(zz))))
        def _():
            sent(p_sem.at[zz])

        return carry

    lax.fori_loop(0, Z, drain, 0)
    for sem, count in ((q_sem, 2 * Z), (sib_sem, 4 * Z)):
        pltpu.make_async_copy(G.at[0:count], G.at[0:count], sem).wait()
    pltpu.make_async_copy(meta.at[0:n_seq - 1], meta.at[0:n_seq - 1], meta_send).wait()
    pltpu.make_async_copy(part.at[0:n_dev - 1], part.at[0:n_dev - 1], part_recv).wait()

    parts = part[...]
    lses, t = parts[:, :n_seq, :], jnp.sum(parts[:, n_seq:2 * n_seq, :], axis=0)
    top = jnp.max(lses, axis=0)
    lse = top + jnp.log(jnp.sum(jnp.exp(lses - top[None]), axis=0))
    keep = jnp.concatenate([meta[i, 1:2, :] for i in range(n_seq)], axis=0).astype(jnp.float32)
    loss = keep * (lse - t)

    def whole(a):
        return jnp.sum(jnp.sum(a, axis=0, keepdims=True), axis=1, keepdims=True)

    count = whole(keep)
    ce_ref[...] = whole(loss) / count
    zr_ref[...] = jnp.sqrt(whole(keep * lse * lse) / count)
    mine = lax.broadcasted_iota(jnp.int32, (n_seq, toks), 0) == s
    done[0:1, :] = jnp.sum(jnp.where(mine, lse, 0.0), axis=0, keepdims=True)
    done[1:2, :] = jnp.sum(jnp.where(mine, t, 0.0), axis=0, keepdims=True)
    out = pltpu.make_async_copy(done, tok_ref, in_sem.at[0])
    out.start()
    out.wait()
    pltpu.make_async_copy(part.at[0:n_dev - 1], part.at[0:n_dev - 1], part_send).wait()


def on_device(n_voc, n_seq, hidden, weight, targets, loss_mask):
    toks, feat = hidden.shape
    sub = 16
    voc, wide = weight.shape
    fits = (
        n_seq == 4 and n_voc % 2 == 0 and n_voc >= 8 and toks == LANES
        and feat % sub == 0 and 2 * feat % LANES == 0 and voc % 8 == 0
    )
    if not fits:
        return general(hidden, weight, targets, loss_mask)
    n_dev = n_voc * n_seq
    n_z = n_voc // 2
    f32 = jnp.float32
    dma = pltpu.SemaphoreType.DMA
    vmem = pl.BlockSpec(memory_space=pltpu.VMEM)
    hbm = pl.BlockSpec(memory_space=pltpu.HBM)
    tok, ce, root = pl.pallas_call(
        functools.partial(kernel, n_voc, n_seq),
        out_shape=(
            jax.ShapeDtypeStruct((2, toks), f32),
            jax.ShapeDtypeStruct((1, 1), f32),
            jax.ShapeDtypeStruct((1, 1), f32),
        ),
        in_specs=[hbm, hbm, hbm, hbm],
        out_specs=(hbm, vmem, vmem),
        scratch_shapes=[
            pltpu.VMEM((n_dev, feat, toks), jnp.bfloat16),
            pltpu.VMEM((voc, wide), jnp.bfloat16),
            pltpu.VMEM((2, voc, 2 * toks), f32),
            pltpu.VMEM((n_seq, 8, LANES), jnp.int32),
            pltpu.VMEM((n_dev, 2 * n_seq, LANES), f32),
            pltpu.VMEM((2, toks), f32),
            dma, dma((3,)), dma((n_dev,)), dma((2, n_z)), dma((2, n_z)),
            dma((n_z,)), dma, dma, dma, dma, dma, dma,
        ],
        compiler_params=pltpu.CompilerParams(
            collective_id=0, has_side_effects=True, vmem_limit_bytes=64 * 2**20
        ),
        cost_estimate=pl.CostEstimate(
            flops=2 * n_seq * toks * wide * voc, bytes_accessed=2 * voc * wide,
            transcendentals=n_seq * toks * voc,
        ),
    )(hidden.T, weight, targets.reshape(1, toks), loss_mask.reshape(1, toks))
    lse = tok[0]
    loss = loss_mask.astype(f32) * (lse - tok[1])
    return (lse, loss, ce.reshape(()), root.reshape(()))


def solution(mesh):
    in_specs = (P("seq", "vocab"), P(("vocab", "seq"), None), P("seq"), P("seq"))
    out_specs = (P("seq"), P("seq"), P(), P())
    return jax.shard_map(
        functools.partial(on_device, mesh.shape["vocab"], mesh.shape["seq"]),
        mesh=mesh, in_specs=in_specs, out_specs=out_specs, check_vma=False,
    )
```

```python
import functools
import jax
import jax.numpy as jnp
from jax import lax
from jax.experimental import pallas as pl
from jax.experimental.pallas import tpu as pltpu
from jax.sharding import PartitionSpec as P

MESH = pl.DeviceIdType.MESH
LANES = 128


def general(hidden, weight, targets, loss_mask):
    voc_local = weight.shape[0]
    all_ids = lax.all_gather(targets, "seq", axis=0, tiled=True)
    hidden = lax.all_gather(hidden, "vocab", axis=1, tiled=True)
    logits = lax.dot_general(
        lax.all_gather(hidden, "seq", axis=0, tiled=True),
        weight,
        (((1,), (1,)), ((), ())),
        preferred_element_type=jnp.float32,
    )
    block_index = lax.axis_index("vocab") * lax.axis_size("seq") + lax.axis_index("seq")
    columns = block_index * voc_local + jnp.arange(voc_local, dtype=jnp.int32)
    target_hit = columns[None, :] == all_ids[:, None]
    target_part = jnp.sum(jnp.where(target_hit, logits, jnp.float32(0.0)), axis=1)
    row_peak = lax.pmax(jnp.max(logits, axis=1), ("vocab", "seq"))
    exp_part = jnp.sum(jnp.exp(logits - row_peak[:, None]), axis=1)
    share_exp, share_target = (
        lax.psum_scatter(exp_part, "seq", scatter_dimension=0, tiled=True),
        lax.psum_scatter(target_part, "seq", scatter_dimension=0, tiled=True),
    )
    exp_total, target_logit = lax.psum((share_exp, share_target), "vocab")
    tok_local = targets.shape[0]
    own_peak = lax.dynamic_slice_in_dim(row_peak, lax.axis_index("seq") * tok_local, tok_local, 0)
    lse = own_peak + jnp.log(exp_total)
    keep = loss_mask.astype(jnp.float32)
    token_loss = keep * (lse - target_logit)
    loss_sum, square_sum, count = lax.psum(
        (jnp.sum(token_loss), jnp.sum(keep * lse * lse), jnp.sum(keep)), "seq"
    )
    return (lse, token_loss, loss_sum / count, jnp.sqrt(square_sum / count))


def kernel(
    n_voc, n_seq,
    h_ref, w_hbm, tgt_ref, msk_ref,
    tok_ref, ce_ref, zr_ref,
    G, W, acc, meta, part, done,
    w_sem, in_sem, recv, up_sem, down_sem, p_sem, q_sem, sib_sem, meta_send, meta_recv, part_send, part_recv,
):
    Z = n_voc // 2
    n_dev = n_voc * n_seq
    v, s = lax.axis_index("vocab"), lax.axis_index("seq")
    z, y, x, c = v // 2, v % 2, s // 2, s % 2
    me = v * n_seq + s
    voc = w_hbm.shape[0]
    feat, toks = h_ref.shape
    H, cut_rows = G.shape[1], G.shape[2]

    own = (
        pltpu.make_async_copy(tgt_ref, meta.at[s, pl.ds(0, 1)], in_sem.at[0]),
        pltpu.make_async_copy(msk_ref, meta.at[s, pl.ds(1, 1)], in_sem.at[1]),
    )
    own += tuple(
        pltpu.make_async_copy(h_ref.at[pl.ds(h * cut_rows, cut_rows)], G.at[me, h], in_sem.at[2 + h])
        for h in range(H)
    )
    for copy in own:
        copy.start()
    load = pltpu.make_async_copy(w_hbm, W, w_sem)
    load.start()

    barrier = pltpu.get_barrier_semaphore()

    def each_other(act):
        def ring(j, carry):
            dv = v + j
            dv = jnp.where(dv >= n_voc, dv - n_voc, dv)
            for k in range(1, n_seq):
                ds = s + k
                act(dv, jnp.where(ds >= n_seq, ds - n_seq, ds))

            @pl.when(j > 0)
            def _():
                act(dv, s)

            return carry

        lax.fori_loop(0, n_voc, ring, 0)

    def greet(dv, ds):
        pl.semaphore_signal(barrier, inc=1, device_id=(dv, ds), device_id_type=MESH)

    each_other(greet)
    for copy in own:
        copy.wait()
    pl.semaphore_wait(barrier, n_dev - 1)

    flip_y, flip_x = 1 - 2 * y, 2 - 4 * x
    sib = s + 1 - 2 * c
    p_v, p_s = v + (1 - c) * flip_y, s + c * flip_x
    q_v, q_s = v + c * flip_y, s + (1 - c) * flip_x

    def block(zz, yy, ss):
        return (2 * zz + yy) * n_seq + ss

    def push(b, h, sem, dv, ds):
        pltpu.make_async_remote_copy(
            src_ref=G.at[b, h], dst_ref=G.at[b, h], send_sem=sem, recv_sem=recv.at[b, h],
            device_id=(dv, ds), device_id_type=MESH,
        ).start()

    def arrived(b, h):
        pltpu.make_async_remote_copy(
            src_ref=G.at[b, h], dst_ref=G.at[b, h], send_sem=sib_sem, recv_sem=recv.at[b, h],
            device_id=(v, sib), device_id_type=MESH,
        ).wait_recv()

    near = jnp.minimum(z, Z - 1 - z)
    far_side = jnp.where(2 * z < Z, 1, -1)

    def order(i):
        in_near = i <= 2 * near
        sgn = jnp.where(in_near, jnp.where(i % 2 == 1, -1, 1), far_side)
        dist = jnp.where(in_near, (i + 1) // 2, i - near)
        return z + sgn * dist

    def to_sib(b, h):
        push(b, h, sib_sem, v, sib)

    def along(b, h, zz, side):
        @pl.when(jnp.logical_and(zz <= z, z + 1 < Z))
        def _():
            push(b, h, up_sem.at[side, zz, h], v + 2, s)

        @pl.when(jnp.logical_and(zz >= z, z > 0))
        def _():
            push(b, h, down_sem.at[side, zz, h], v - 2, s)

    def is_end(zz):
        return jnp.logical_or(zz == 0, zz == Z - 1)

    def line(zz, h):
        b = block(zz, y, s)
        along(b, h, zz, 0)

        @pl.when(jnp.logical_or(zz == z, jnp.logical_not(is_end(zz))))
        def _():
            push(b, h, p_sem.at[zz, h], p_v, p_s)

        push(b, h, q_sem, q_v, q_s)
        to_sib(b, h)

    for h in range(H):
        line(z, h)

    def tell(i, carry):
        d = lax.rem(s + i, n_seq)
        pltpu.make_async_remote_copy(
            src_ref=meta.at[s], dst_ref=meta.at[s], send_sem=meta_send, recv_sem=meta_recv,
            device_id=(v, d), device_id_type=MESH,
        ).start()
        return carry

    lax.fori_loop(1, n_seq, tell, 0)

    p_y, q_y = p_v % 2, q_v % 2

    def from_p(zz, h):
        b = block(zz, p_y, p_s)
        arrived(b, h)

        @pl.when(is_end(zz))
        def _():
            along(b, h, zz, 1)

        push(b, h, q_sem, q_v, q_s)
        to_sib(b, h)

    def from_q(zz, h, yy, ss):
        b = block(zz, yy, ss)
        arrived(b, h)
        to_sib(b, h)

    def chunk(zz, xx):
        sides = []
        for cc in range(2):
            pair = [G[block(zz, yy, 2 * xx + cc), h] for yy in range(2) for h in range(H)]
            sides.append(jnp.concatenate(pair, axis=0))
        rows = jnp.concatenate(sides, axis=1)
        cols = pl.ds(pl.multiple_of(zz * 2 * feat, LANES), 2 * feat)
        acc[xx] += lax.dot_general(
            W[:, cols], rows, (((1,), (0,)), ((), ())), preferred_element_type=jnp.float32
        )

    step = max(r for r in range(8, 257, 8) if voc % r == 0)

    def finish(xx):
        ids = jnp.concatenate([meta[2 * xx, 0:1, :], meta[2 * xx + 1, 0:1, :]], axis=1)
        ids = ids - me * voc
        wide = (8, 2 * toks)

        def peak(r, m):
            tile = acc[xx, pl.ds(pl.multiple_of(r * step, 8), step), :]
            return jnp.maximum(m, jnp.max(tile.reshape(step // 8, 8, 2 * toks), axis=0))

        m = lax.fori_loop(0, voc // step, peak, jnp.full(wide, -jnp.inf, jnp.float32))
        m = jnp.max(m, axis=0, keepdims=True)

        def total(r, carry):
            e, t = carry
            tile = acc[xx, pl.ds(pl.multiple_of(r * step, 8), step), :]
            row = lax.broadcasted_iota(jnp.int32, (step, 2 * toks), 0) + r * step
            hit = jnp.where(row == ids, tile, jnp.float32(0.0))
            e += jnp.sum(jnp.exp(tile - m).reshape(step // 8, 8, 2 * toks), axis=0)
            t += jnp.sum(hit.reshape(step // 8, 8, 2 * toks), axis=0)
            return e, t

        zero = jnp.zeros(wide, jnp.float32)
        e, t = lax.fori_loop(0, voc // step, total, (zero, zero))
        lse = m + jnp.log(jnp.sum(e, axis=0, keepdims=True))
        t = jnp.sum(t, axis=0, keepdims=True)
        for cc in range(2):
            cut = slice(cc * toks, (cc + 1) * toks)
            part[me, pl.ds(2 * xx + cc, 1), :] = lse[:, cut]
            part[me, pl.ds(n_seq + 2 * xx + cc, 1), :] = t[:, cut]

    def do_chunk(k):
        zz, far = order(k % Z), k // Z
        xx = x + far * (1 - 2 * x)
        ss = 2 * xx + 1 - c
        for yy in range(2):
            for h in range(H):
                arrived(block(zz, yy, ss), h)
        chunk(zz, xx)

    acc[...] = jnp.zeros_like(acc)
    items = H * Z

    def turn(t, carry):
        @pl.when(t < items)
        def _():
            zz, h = order(t // H), t % H
            arrived(block(zz, y, s), h)
            line(zz, h)

        k = t - 1

        @pl.when(jnp.logical_and(k >= H, k < items))
        def _():
            from_p(order(k // H), k % H)

        j = t - 2

        @pl.when(jnp.logical_and(j >= 1, j < items))
        def _():
            from_q(order(j // H), j % H, q_y, q_s)

        i = t - 3

        @pl.when(jnp.logical_and(i >= 0, i < items))
        def _():
            from_q(order(i // H), i % H, 1 - y, s + flip_x)

        @pl.when(t == 2 * H)
        def _():
            load.wait()

        g = t - 2 * H

        @pl.when(jnp.logical_and(g >= 0, jnp.logical_and(g % H == 0, g // H < Z)))
        def _():
            do_chunk(g // H)

        f = t - 2 * H - 1

        @pl.when(jnp.logical_and(f >= 0, jnp.logical_and(f % H == 0, f // H < Z - 1)))
        def _():
            do_chunk(Z + f // H)

        return carry

    for h in range(H):
        from_p(z, h)
    from_q(z, 0, q_y, q_s)
    lax.fori_loop(H, items + 3, turn, 0)
    pltpu.make_async_copy(meta.at[0:n_seq - 1], meta.at[0:n_seq - 1], meta_recv).wait()
    finish(x)
    do_chunk(2 * Z - 1)
    finish(1 - x)

    def share(dv, ds):
        pltpu.make_async_remote_copy(
            src_ref=part.at[me], dst_ref=part.at[me], send_sem=part_send, recv_sem=part_recv,
            device_id=(dv, ds), device_id_type=MESH,
        ).start()

    each_other(share)

    def sent(sem):
        pltpu.make_async_copy(G.at[0, 0], G.at[0, 0], sem).wait()

    def drain(zz, carry):
        for h in range(H):
            for side in range(2):
                also = True if side == 0 else is_end(zz)

                @pl.when(jnp.logical_and(also, jnp.logical_and(zz <= z, z + 1 < Z)))
                def _():
                    sent(up_sem.at[side, zz, h])

                @pl.when(jnp.logical_and(also, jnp.logical_and(zz >= z, z > 0)))
                def _():
                    sent(down_sem.at[side, zz, h])

            @pl.when(jnp.logical_or(zz == z, jnp.logical_not(is_end(zz))))
            def _():
                sent(p_sem.at[zz, h])

        return carry

    lax.fori_loop(0, Z, drain, 0)
    for sem, count in ((q_sem, 2 * Z), (sib_sem, 4 * Z)):
        pltpu.make_async_copy(G.at[0:count], G.at[0:count], sem).wait()
    pltpu.make_async_copy(meta.at[0:n_seq - 1], meta.at[0:n_seq - 1], meta_send).wait()
    pltpu.make_async_copy(part.at[0:n_dev - 1], part.at[0:n_dev - 1], part_recv).wait()

    parts = part[...]
    lses, t = parts[:, :n_seq, :], jnp.sum(parts[:, n_seq:2 * n_seq, :], axis=0)
    top = jnp.max(lses, axis=0)
    lse = top + jnp.log(jnp.sum(jnp.exp(lses - top[None]), axis=0))
    keep = jnp.concatenate([meta[i, 1:2, :] for i in range(n_seq)], axis=0).astype(jnp.float32)
    loss = keep * (lse - t)

    def whole(a):
        return jnp.sum(jnp.sum(a, axis=0, keepdims=True), axis=1, keepdims=True)

    count = whole(keep)
    ce_ref[...] = whole(loss) / count
    zr_ref[...] = jnp.sqrt(whole(keep * lse * lse) / count)
    mine = lax.broadcasted_iota(jnp.int32, (n_seq, toks), 0) == s
    done[0:1, :] = jnp.sum(jnp.where(mine, lse, 0.0), axis=0, keepdims=True)
    done[1:2, :] = jnp.sum(jnp.where(mine, t, 0.0), axis=0, keepdims=True)
    out = pltpu.make_async_copy(done, tok_ref, in_sem.at[0])
    out.start()
    out.wait()
    pltpu.make_async_copy(part.at[0:n_dev - 1], part.at[0:n_dev - 1], part_send).wait()


def on_device(n_voc, n_seq, hidden, weight, targets, loss_mask):
    toks, feat = hidden.shape
    sub, pieces = 16, 2
    voc, wide = weight.shape
    fits = (
        n_seq == 4 and n_voc % 2 == 0 and n_voc >= 8 and toks == LANES
        and feat % (sub * pieces) == 0 and 2 * feat % LANES == 0 and voc % 8 == 0
    )
    if not fits:
        return general(hidden, weight, targets, loss_mask)
    n_dev = n_voc * n_seq
    n_z = n_voc // 2
    f32 = jnp.float32
    dma = pltpu.SemaphoreType.DMA
    vmem = pl.BlockSpec(memory_space=pltpu.VMEM)
    hbm = pl.BlockSpec(memory_space=pltpu.HBM)
    tok, ce, root = pl.pallas_call(
        functools.partial(kernel, n_voc, n_seq),
        out_shape=(
            jax.ShapeDtypeStruct((2, toks), f32),
            jax.ShapeDtypeStruct((1, 1), f32),
            jax.ShapeDtypeStruct((1, 1), f32),
        ),
        in_specs=[hbm, hbm, hbm, hbm],
        out_specs=(hbm, vmem, vmem),
        scratch_shapes=[
            pltpu.VMEM((n_dev, pieces, feat // pieces, toks), jnp.bfloat16),
            pltpu.VMEM((voc, wide), jnp.bfloat16),
            pltpu.VMEM((2, voc, 2 * toks), f32),
            pltpu.VMEM((n_seq, 8, LANES), jnp.int32),
            pltpu.VMEM((n_dev, 2 * n_seq, LANES), f32),
            pltpu.VMEM((2, toks), f32),
            dma, dma((2 + pieces,)), dma((n_dev, pieces)), dma((2, n_z, pieces)), dma((2, n_z, pieces)),
            dma((n_z, pieces)), dma, dma, dma, dma, dma, dma,
        ],
        compiler_params=pltpu.CompilerParams(
            collective_id=0, has_side_effects=True, vmem_limit_bytes=64 * 2**20
        ),
        cost_estimate=pl.CostEstimate(
            flops=2 * n_seq * toks * wide * voc, bytes_accessed=2 * voc * wide,
            transcendentals=n_seq * toks * voc,
        ),
    )(hidden.T, weight, targets.reshape(1, toks), loss_mask.reshape(1, toks))
    lse = tok[0]
    loss = loss_mask.astype(f32) * (lse - tok[1])
    return (lse, loss, ce.reshape(()), root.reshape(()))


def solution(mesh):
    in_specs = (P("seq", "vocab"), P(("vocab", "seq"), None), P("seq"), P("seq"))
    out_specs = (P("seq"), P("seq"), P(), P())
    return jax.shard_map(
        functools.partial(on_device, mesh.shape["vocab"], mesh.shape["seq"]),
        mesh=mesh, in_specs=in_specs, out_specs=out_specs, check_vma=False,
    )
```

```python
import functools
import jax
import jax.numpy as jnp
from jax import lax
from jax.experimental import pallas as pl
from jax.experimental.pallas import tpu as pltpu
from jax.sharding import PartitionSpec as P

MESH = pl.DeviceIdType.MESH
LANES = 128


def general(hidden, weight, targets, loss_mask):
    voc_local = weight.shape[0]
    all_ids = lax.all_gather(targets, "seq", axis=0, tiled=True)
    hidden = lax.all_gather(hidden, "vocab", axis=1, tiled=True)
    logits = lax.dot_general(
        lax.all_gather(hidden, "seq", axis=0, tiled=True),
        weight,
        (((1,), (1,)), ((), ())),
        preferred_element_type=jnp.float32,
    )
    block_index = lax.axis_index("vocab") * lax.axis_size("seq") + lax.axis_index("seq")
    columns = block_index * voc_local + jnp.arange(voc_local, dtype=jnp.int32)
    target_hit = columns[None, :] == all_ids[:, None]
    target_part = jnp.sum(jnp.where(target_hit, logits, jnp.float32(0.0)), axis=1)
    row_peak = lax.pmax(jnp.max(logits, axis=1), ("vocab", "seq"))
    exp_part = jnp.sum(jnp.exp(logits - row_peak[:, None]), axis=1)
    share_exp, share_target = (
        lax.psum_scatter(exp_part, "seq", scatter_dimension=0, tiled=True),
        lax.psum_scatter(target_part, "seq", scatter_dimension=0, tiled=True),
    )
    exp_total, target_logit = lax.psum((share_exp, share_target), "vocab")
    tok_local = targets.shape[0]
    own_peak = lax.dynamic_slice_in_dim(row_peak, lax.axis_index("seq") * tok_local, tok_local, 0)
    lse = own_peak + jnp.log(exp_total)
    keep = loss_mask.astype(jnp.float32)
    token_loss = keep * (lse - target_logit)
    loss_sum, square_sum, count = lax.psum(
        (jnp.sum(token_loss), jnp.sum(keep * lse * lse), jnp.sum(keep)), "seq"
    )
    return (lse, token_loss, loss_sum / count, jnp.sqrt(square_sum / count))


def kernel(
    n_voc, n_seq,
    h_ref, w_hbm, tgt_ref, msk_ref,
    tok_ref, ce_ref, zr_ref,
    G, W, acc, meta, part, got, terms, done,
    w_sem, in_sem, recv, up_sem, down_sem, p_sem, q_sem, sib_sem, meta_send, meta_recv, part_send, part_recv, term_send, term_recv,
):
    Z = n_voc // 2
    n_dev = n_voc * n_seq
    v, s = lax.axis_index("vocab"), lax.axis_index("seq")
    z, y, x, c = v // 2, v % 2, s // 2, s % 2
    me = v * n_seq + s
    voc = w_hbm.shape[0]
    feat, toks = h_ref.shape
    H, cut_rows = G.shape[1], G.shape[2]

    own = (
        pltpu.make_async_copy(tgt_ref, meta.at[s, pl.ds(0, 1)], in_sem.at[0]),
        pltpu.make_async_copy(msk_ref, meta.at[s, pl.ds(1, 1)], in_sem.at[1]),
    )
    own += tuple(
        pltpu.make_async_copy(h_ref.at[pl.ds(h * cut_rows, cut_rows)], G.at[me, h], in_sem.at[2 + h])
        for h in range(H)
    )
    for copy in own:
        copy.start()
    load = pltpu.make_async_copy(w_hbm, W, w_sem)
    load.start()

    barrier = pltpu.get_barrier_semaphore()

    def each_other(act):
        def ring(j, carry):
            dv = v + j
            dv = jnp.where(dv >= n_voc, dv - n_voc, dv)
            for k in range(1, n_seq):
                ds = s + k
                act(dv, jnp.where(ds >= n_seq, ds - n_seq, ds))

            @pl.when(j > 0)
            def _():
                act(dv, s)

            return carry

        lax.fori_loop(0, n_voc, ring, 0)

    def greet(dv, ds):
        pl.semaphore_signal(barrier, inc=1, device_id=(dv, ds), device_id_type=MESH)

    each_other(greet)
    for copy in own:
        copy.wait()
    pl.semaphore_wait(barrier, n_dev - 1)

    flip_y, flip_x = 1 - 2 * y, 2 - 4 * x
    sib = s + 1 - 2 * c
    p_v, p_s = v + (1 - c) * flip_y, s + c * flip_x
    q_v, q_s = v + c * flip_y, s + (1 - c) * flip_x

    def block(zz, yy, ss):
        return (2 * zz + yy) * n_seq + ss

    def push(b, h, sem, dv, ds):
        pltpu.make_async_remote_copy(
            src_ref=G.at[b, h], dst_ref=G.at[b, h], send_sem=sem, recv_sem=recv.at[b, h],
            device_id=(dv, ds), device_id_type=MESH,
        ).start()

    def arrived(b, h):
        pltpu.make_async_remote_copy(
            src_ref=G.at[b, h], dst_ref=G.at[b, h], send_sem=sib_sem, recv_sem=recv.at[b, h],
            device_id=(v, sib), device_id_type=MESH,
        ).wait_recv()

    near = jnp.minimum(z, Z - 1 - z)
    far_side = jnp.where(2 * z < Z, 1, -1)

    def order(i):
        in_near = i <= 2 * near
        sgn = jnp.where(in_near, jnp.where(i % 2 == 1, -1, 1), far_side)
        dist = jnp.where(in_near, (i + 1) // 2, i - near)
        return z + sgn * dist

    def to_sib(b, h):
        push(b, h, sib_sem, v, sib)

    def along(b, h, zz, side):
        @pl.when(jnp.logical_and(zz <= z, z + 1 < Z))
        def _():
            push(b, h, up_sem.at[side, zz, h], v + 2, s)

        @pl.when(jnp.logical_and(zz >= z, z > 0))
        def _():
            push(b, h, down_sem.at[side, zz, h], v - 2, s)

    def is_end(zz):
        return jnp.logical_or(zz == 0, zz == Z - 1)

    def line(zz, h):
        b = block(zz, y, s)
        along(b, h, zz, 0)

        @pl.when(jnp.logical_or(zz == z, jnp.logical_not(is_end(zz))))
        def _():
            push(b, h, p_sem.at[zz, h], p_v, p_s)

        push(b, h, q_sem, q_v, q_s)
        to_sib(b, h)

    for h in range(H):
        line(z, h)

    def tell(i, carry):
        d = lax.rem(s + i, n_seq)
        pltpu.make_async_remote_copy(
            src_ref=meta.at[s], dst_ref=meta.at[s], send_sem=meta_send, recv_sem=meta_recv,
            device_id=(v, d), device_id_type=MESH,
        ).start()
        return carry

    lax.fori_loop(1, n_seq, tell, 0)

    p_y, q_y = p_v % 2, q_v % 2

    def from_p(zz, h):
        b = block(zz, p_y, p_s)
        arrived(b, h)

        @pl.when(is_end(zz))
        def _():
            along(b, h, zz, 1)

        push(b, h, q_sem, q_v, q_s)
        to_sib(b, h)

    def from_q(zz, h, yy, ss):
        b = block(zz, yy, ss)
        arrived(b, h)
        to_sib(b, h)

    def chunk(zz, xx):
        sides = []
        for cc in range(2):
            pair = [G[block(zz, yy, 2 * xx + cc), h] for yy in range(2) for h in range(H)]
            sides.append(jnp.concatenate(pair, axis=0))
        rows = jnp.concatenate(sides, axis=1)
        cols = pl.ds(pl.multiple_of(zz * 2 * feat, LANES), 2 * feat)
        acc[xx] += lax.dot_general(
            W[:, cols], rows, (((1,), (0,)), ((), ())), preferred_element_type=jnp.float32
        )

    step = max(r for r in range(8, 257, 8) if voc % r == 0)

    def finish(xx):
        ids = jnp.concatenate([meta[2 * xx, 0:1, :], meta[2 * xx + 1, 0:1, :]], axis=1)
        ids = ids - me * voc
        wide = (8, 2 * toks)

        def peak(r, m):
            tile = acc[xx, pl.ds(pl.multiple_of(r * step, 8), step), :]
            return jnp.maximum(m, jnp.max(tile.reshape(step // 8, 8, 2 * toks), axis=0))

        m = lax.fori_loop(0, voc // step, peak, jnp.full(wide, -jnp.inf, jnp.float32))
        m = jnp.max(m, axis=0, keepdims=True)

        def total(r, carry):
            e, t = carry
            tile = acc[xx, pl.ds(pl.multiple_of(r * step, 8), step), :]
            row = lax.broadcasted_iota(jnp.int32, (step, 2 * toks), 0) + r * step
            hit = jnp.where(row == ids, tile, jnp.float32(0.0))
            e += jnp.sum(jnp.exp(tile - m).reshape(step // 8, 8, 2 * toks), axis=0)
            t += jnp.sum(hit.reshape(step // 8, 8, 2 * toks), axis=0)
            return e, t

        zero = jnp.zeros(wide, jnp.float32)
        e, t = lax.fori_loop(0, voc // step, total, (zero, zero))
        lse = m + jnp.log(jnp.sum(e, axis=0, keepdims=True))
        t = jnp.sum(t, axis=0, keepdims=True)
        for cc in range(2):
            cut = slice(cc * toks, (cc + 1) * toks)
            part[2 * xx + cc, 0:1, :] = lse[:, cut]
            part[2 * xx + cc, 1:2, :] = t[:, cut]

    def do_chunk(k):
        zz, far = order(k % Z), k // Z
        xx = x + far * (1 - 2 * x)
        ss = 2 * xx + 1 - c
        for yy in range(2):
            for h in range(H):
                arrived(block(zz, yy, ss), h)
        chunk(zz, xx)

    acc[...] = jnp.zeros_like(acc)

    def turn(r, carry):
        @pl.when(r < Z)
        def _():
            for h in range(H):
                arrived(block(order(r), y, s), h)
                line(order(r), h)

        @pl.when(r <= Z)
        def _():
            for h in range(H):
                from_p(order(r - 1), h)

        @pl.when(jnp.logical_and(r >= 2, r < Z + 2))
        def _():
            for h in range(H):
                from_q(order(r - 2), h, q_y, q_s)

        @pl.when(r == 3)
        def _():
            load.wait()
            pltpu.make_async_copy(meta.at[0:n_seq - 1], meta.at[0:n_seq - 1], meta_recv).wait()

        @pl.when(r >= 3)
        def _():
            do_chunk(r - 3)

        @pl.when(r == Z + 2)
        def _():
            finish(x)

        @pl.when(r >= 3)
        def _():
            for h in range(H):
                from_q(order(r - 3), h, 1 - y, s + flip_x)

        @pl.when(r >= 4)
        def _():
            do_chunk(Z + r - 4)

        return carry

    lax.fori_loop(1, Z + 3, turn, 0)
    do_chunk(2 * Z - 1)
    finish(1 - x)

    def share(dv, ds):
        pltpu.make_async_remote_copy(
            src_ref=part.at[ds], dst_ref=got.at[me], send_sem=part_send, recv_sem=part_recv,
            device_id=(dv, ds), device_id_type=MESH,
        ).start()

    each_other(share)
    got[me] = part[s]

    def sent(sem):
        pltpu.make_async_copy(G.at[0, 0], G.at[0, 0], sem).wait()

    def drain(zz, carry):
        for h in range(H):
            for side in range(2):
                also = True if side == 0 else is_end(zz)

                @pl.when(jnp.logical_and(also, jnp.logical_and(zz <= z, z + 1 < Z)))
                def _():
                    sent(up_sem.at[side, zz, h])

                @pl.when(jnp.logical_and(also, jnp.logical_and(zz >= z, z > 0)))
                def _():
                    sent(down_sem.at[side, zz, h])

            @pl.when(jnp.logical_or(zz == z, jnp.logical_not(is_end(zz))))
            def _():
                sent(p_sem.at[zz, h])

        return carry

    lax.fori_loop(0, Z, drain, 0)
    for sem, count in ((q_sem, 2 * Z), (sib_sem, 4 * Z)):
        pltpu.make_async_copy(G.at[0:count], G.at[0:count], sem).wait()
    pltpu.make_async_copy(meta.at[0:n_seq - 1], meta.at[0:n_seq - 1], meta_send).wait()
    pltpu.make_async_copy(got.at[0:n_dev - 1], got.at[0:n_dev - 1], part_recv).wait()

    lses = got[:, 0, :]
    t = jnp.sum(got[:, 1, :], axis=0, keepdims=True)
    top = jnp.max(lses, axis=0, keepdims=True)
    lse = top + jnp.log(jnp.sum(jnp.exp(lses - top), axis=0, keepdims=True))
    mine = meta[s, 1:2, :].astype(jnp.float32)
    terms[s, 0:1, :] = mine * (lse - t)
    terms[s, 1:2, :] = mine * lse * lse

    def pass_on(i, carry):
        pltpu.make_async_remote_copy(
            src_ref=terms.at[s], dst_ref=terms.at[s], send_sem=term_send, recv_sem=term_recv,
            device_id=(v, lax.rem(s + i, n_seq)), device_id_type=MESH,
        ).start()
        return carry

    lax.fori_loop(1, n_seq, pass_on, 0)
    done[0:1, :] = lse
    done[1:2, :] = t
    out = pltpu.make_async_copy(done, tok_ref, in_sem.at[0])
    out.start()

    def whole(a):
        return jnp.sum(jnp.sum(a, axis=0, keepdims=True), axis=1, keepdims=True)

    count = whole(meta[:, 1, :].astype(jnp.float32))
    pltpu.make_async_copy(got.at[0:n_dev - 1], got.at[0:n_dev - 1], part_send).wait()
    pltpu.make_async_copy(terms.at[0:n_seq - 1], terms.at[0:n_seq - 1], term_recv).wait()
    ce_ref[...] = whole(terms[:, 0, :]) / count
    zr_ref[...] = jnp.sqrt(whole(terms[:, 1, :]) / count)
    pltpu.make_async_copy(terms.at[0:n_seq - 1], terms.at[0:n_seq - 1], term_send).wait()
    out.wait()


def on_device(n_voc, n_seq, hidden, weight, targets, loss_mask):
    toks, feat = hidden.shape
    sub, pieces = 16, 1
    voc, wide = weight.shape
    fits = (
        n_seq == 4 and n_voc % 2 == 0 and n_voc >= 8 and toks == LANES
        and feat % (sub * pieces) == 0 and 2 * feat % LANES == 0 and voc % 8 == 0
    )
    if not fits:
        return general(hidden, weight, targets, loss_mask)
    n_dev = n_voc * n_seq
    n_z = n_voc // 2
    f32 = jnp.float32
    dma = pltpu.SemaphoreType.DMA
    vmem = pl.BlockSpec(memory_space=pltpu.VMEM)
    hbm = pl.BlockSpec(memory_space=pltpu.HBM)
    tok, ce, root = pl.pallas_call(
        functools.partial(kernel, n_voc, n_seq),
        out_shape=(
            jax.ShapeDtypeStruct((2, toks), f32),
            jax.ShapeDtypeStruct((1, 1), f32),
            jax.ShapeDtypeStruct((1, 1), f32),
        ),
        in_specs=[hbm, hbm, hbm, hbm],
        out_specs=(hbm, vmem, vmem),
        scratch_shapes=[
            pltpu.VMEM((n_dev, pieces, feat // pieces, toks), jnp.bfloat16),
            pltpu.VMEM((voc, wide), jnp.bfloat16),
            pltpu.VMEM((2, voc, 2 * toks), f32),
            pltpu.VMEM((n_seq, 8, LANES), jnp.int32),
            pltpu.VMEM((n_seq, 2, toks), f32),
            pltpu.VMEM((n_dev, 2, toks), f32),
            pltpu.VMEM((n_seq, 2, toks), f32),
            pltpu.VMEM((2, toks), f32),
            dma, dma((2 + pieces,)), dma((n_dev, pieces)), dma((2, n_z, pieces)), dma((2, n_z, pieces)),
            dma((n_z, pieces)), dma, dma, dma, dma, dma, dma, dma, dma,
        ],
        compiler_params=pltpu.CompilerParams(
            collective_id=0, has_side_effects=True, vmem_limit_bytes=64 * 2**20
        ),
        cost_estimate=pl.CostEstimate(
            flops=2 * n_seq * toks * wide * voc, bytes_accessed=2 * voc * wide,
            transcendentals=n_seq * toks * voc,
        ),
    )(hidden.T, weight, targets.reshape(1, toks), loss_mask.reshape(1, toks))
    lse = tok[0]
    loss = loss_mask.astype(f32) * (lse - tok[1])
    return (lse, loss, ce.reshape(()), root.reshape(()))


def solution(mesh):
    in_specs = (P("seq", "vocab"), P(("vocab", "seq"), None), P("seq"), P("seq"))
    out_specs = (P("seq"), P("seq"), P(), P())
    return jax.shard_map(
        functools.partial(on_device, mesh.shape["vocab"], mesh.shape["seq"]),
        mesh=mesh, in_specs=in_specs, out_specs=out_specs, check_vma=False,
    )
```

```python
import functools
import jax
import jax.numpy as jnp
from jax import lax
from jax.experimental import pallas as pl
from jax.experimental.pallas import tpu as pltpu
from jax.sharding import PartitionSpec as P

MESH = pl.DeviceIdType.MESH
LANES = 128


def general(hidden, weight, targets, loss_mask):
    voc_local = weight.shape[0]
    all_ids = lax.all_gather(targets, "seq", axis=0, tiled=True)
    hidden = lax.all_gather(hidden, "vocab", axis=1, tiled=True)
    logits = lax.dot_general(
        lax.all_gather(hidden, "seq", axis=0, tiled=True),
        weight,
        (((1,), (1,)), ((), ())),
        preferred_element_type=jnp.float32,
    )
    block_index = lax.axis_index("vocab") * lax.axis_size("seq") + lax.axis_index("seq")
    columns = block_index * voc_local + jnp.arange(voc_local, dtype=jnp.int32)
    target_hit = columns[None, :] == all_ids[:, None]
    target_part = jnp.sum(jnp.where(target_hit, logits, jnp.float32(0.0)), axis=1)
    row_peak = lax.pmax(jnp.max(logits, axis=1), ("vocab", "seq"))
    exp_part = jnp.sum(jnp.exp(logits - row_peak[:, None]), axis=1)
    share_exp, share_target = (
        lax.psum_scatter(exp_part, "seq", scatter_dimension=0, tiled=True),
        lax.psum_scatter(target_part, "seq", scatter_dimension=0, tiled=True),
    )
    exp_total, target_logit = lax.psum((share_exp, share_target), "vocab")
    tok_local = targets.shape[0]
    own_peak = lax.dynamic_slice_in_dim(row_peak, lax.axis_index("seq") * tok_local, tok_local, 0)
    lse = own_peak + jnp.log(exp_total)
    keep = loss_mask.astype(jnp.float32)
    token_loss = keep * (lse - target_logit)
    loss_sum, square_sum, count = lax.psum(
        (jnp.sum(token_loss), jnp.sum(keep * lse * lse), jnp.sum(keep)), "seq"
    )
    return (lse, token_loss, loss_sum / count, jnp.sqrt(square_sum / count))


def kernel(
    n_voc, n_seq,
    h_ref, w_hbm, tgt_ref, msk_ref,
    tok_ref, ce_ref, zr_ref,
    G, W, acc, meta, part, done,
    w_sem, in_sem, recv, up_sem, down_sem, p_sem, q_sem, sib_sem, meta_send, meta_recv, part_send, part_recv,
):
    Z = n_voc // 2
    n_dev = n_voc * n_seq
    v, s = lax.axis_index("vocab"), lax.axis_index("seq")
    z, y, x, c = v // 2, v % 2, s // 2, s % 2
    me = v * n_seq + s
    voc = w_hbm.shape[0]
    feat, toks = h_ref.shape

    own = (
        pltpu.make_async_copy(h_ref, G.at[me], in_sem.at[0]),
        pltpu.make_async_copy(tgt_ref, meta.at[s, pl.ds(0, 1)], in_sem.at[1]),
        pltpu.make_async_copy(msk_ref, meta.at[s, pl.ds(1, 1)], in_sem.at[2]),
    )
    for copy in own:
        copy.start()
    load = pltpu.make_async_copy(w_hbm, W, w_sem)
    load.start()

    barrier = pltpu.get_barrier_semaphore()

    def greet(i, carry):
        d = lax.rem(me + i, n_dev)
        pl.semaphore_signal(barrier, inc=1, device_id=(d // n_seq, d % n_seq), device_id_type=MESH)
        return carry

    lax.fori_loop(1, n_dev, greet, 0)

    for copy in own:
        copy.wait()
    pl.semaphore_wait(barrier, n_dev - 1)

    flip_y, flip_x = 1 - 2 * y, 2 - 4 * x
    sib = s + 1 - 2 * c
    p_v, p_s = v + (1 - c) * flip_y, s + c * flip_x
    q_v, q_s = v + c * flip_y, s + (1 - c) * flip_x

    def block(zz, yy, ss):
        return (2 * zz + yy) * n_seq + ss

    def push(b, sem, dv, ds):
        pltpu.make_async_remote_copy(
            src_ref=G.at[b], dst_ref=G.at[b], send_sem=sem, recv_sem=recv.at[b],
            device_id=(dv, ds), device_id_type=MESH,
        ).start()

    def arrived(b):
        pltpu.make_async_remote_copy(
            src_ref=G.at[b], dst_ref=G.at[b], send_sem=sib_sem, recv_sem=recv.at[b],
            device_id=(v, sib), device_id_type=MESH,
        ).wait_recv()

    near = jnp.minimum(z, Z - 1 - z)
    far_side = jnp.where(2 * z < Z, 1, -1)

    def order(i):
        in_near = i <= 2 * near
        sgn = jnp.where(in_near, jnp.where(i % 2 == 1, -1, 1), far_side)
        dist = jnp.where(in_near, (i + 1) // 2, i - near)
        return z + sgn * dist

    def to_sib(b):
        push(b, sib_sem, v, sib)

    def along(b, zz, side):
        @pl.when(jnp.logical_and(zz <= z, z + 1 < Z))
        def _():
            push(b, up_sem.at[side, zz], v + 2, s)

        @pl.when(jnp.logical_and(zz >= z, z > 0))
        def _():
            push(b, down_sem.at[side, zz], v - 2, s)

    def by_z(zz):
        return zz != Z // 2

    def line(zz):
        b = block(zz, y, s)
        along(b, zz, 0)

        @pl.when(jnp.logical_or(zz == z, jnp.logical_not(by_z(zz))))
        def _():
            push(b, p_sem.at[zz], p_v, p_s)

        push(b, q_sem, q_v, q_s)
        to_sib(b)

    line(z)

    def tell(i, carry):
        d = lax.rem(s + i, n_seq)
        pltpu.make_async_remote_copy(
            src_ref=meta.at[s], dst_ref=meta.at[s], send_sem=meta_send, recv_sem=meta_recv,
            device_id=(v, d), device_id_type=MESH,
        ).start()
        return carry

    lax.fori_loop(1, n_seq, tell, 0)

    p_y, q_y = p_v % 2, q_v % 2

    def from_p(zz):
        b = block(zz, p_y, p_s)
        arrived(b)

        @pl.when(by_z(zz))
        def _():
            along(b, zz, 1)

        push(b, q_sem, q_v, q_s)
        to_sib(b)

    def from_q(zz, yy, ss):
        b = block(zz, yy, ss)
        arrived(b)
        to_sib(b)

    def chunk(zz, xx, first):
        sides = []
        for cc in range(2):
            pair = [G[block(zz, yy, 2 * xx + cc)] for yy in range(2)]
            sides.append(jnp.concatenate(pair, axis=0))
        rows = jnp.concatenate(sides, axis=1)
        cols = pl.ds(pl.multiple_of(zz * 2 * feat, LANES), 2 * feat)
        out = lax.dot_general(
            W[:, cols], rows, (((1,), (0,)), ((), ())), preferred_element_type=jnp.float32
        )

        @pl.when(first)
        def _():
            acc[xx] = out

        @pl.when(jnp.logical_not(first))
        def _():
            acc[xx] += out

    step = max(r for r in range(8, 257, 8) if voc % r == 0)

    def finish(xx):
        ids = jnp.concatenate([meta[2 * xx, 0:1, :], meta[2 * xx + 1, 0:1, :]], axis=1)
        ids = ids - me * voc
        wide = (8, 2 * toks)

        def peak(r, m):
            tile = acc[xx, pl.ds(pl.multiple_of(r * step, 8), step), :]
            return jnp.maximum(m, jnp.max(tile.reshape(step // 8, 8, 2 * toks), axis=0))

        m = lax.fori_loop(0, voc // step, peak, jnp.full(wide, -jnp.inf, jnp.float32))
        m = jnp.max(m, axis=0, keepdims=True)

        def total(r, carry):
            e, t = carry
            tile = acc[xx, pl.ds(pl.multiple_of(r * step, 8), step), :]
            row = lax.broadcasted_iota(jnp.int32, (step, 2 * toks), 0) + r * step
            hit = jnp.where(row == ids, tile, jnp.float32(0.0))
            e += jnp.sum(jnp.exp(tile - m).reshape(step // 8, 8, 2 * toks), axis=0)
            t += jnp.sum(hit.reshape(step // 8, 8, 2 * toks), axis=0)
            return e, t

        zero = jnp.zeros(wide, jnp.float32)
        e, t = lax.fori_loop(0, voc // step, total, (zero, zero))
        lse = m + jnp.log(jnp.sum(e, axis=0, keepdims=True))
        t = jnp.sum(t, axis=0, keepdims=True)
        for cc in range(2):
            cut = slice(cc * toks, (cc + 1) * toks)
            part[me, pl.ds(2 * xx + cc, 1), :] = lse[:, cut]
            part[me, pl.ds(n_seq + 2 * xx + cc, 1), :] = t[:, cut]

    def do_chunk(k):
        zz, far = order(k % Z), k // Z
        xx = x + far * (1 - 2 * x)
        ss = 2 * xx + 1 - c
        arrived(block(zz, 0, ss))
        arrived(block(zz, 1, ss))
        chunk(zz, xx, k % Z == 0)

    def turn(r, carry):
        @pl.when(r < Z)
        def _():
            zz = order(r)
            arrived(block(zz, y, s))
            line(zz)

        @pl.when(r <= Z)
        def _():
            from_p(order(r - 1))

        @pl.when(jnp.logical_and(r >= 2, r < Z + 2))
        def _():
            from_q(order(r - 2), q_y, q_s)

        @pl.when(r == 3)
        def _():
            load.wait()

        @pl.when(r >= 3)
        def _():
            from_q(order(r - 3), 1 - y, s + flip_x)
            do_chunk(r - 3)

        @pl.when(r >= 4)
        def _():
            do_chunk(Z + r - 4)

        return carry

    lax.fori_loop(1, Z + 3, turn, 0)
    pltpu.make_async_copy(meta.at[0:n_seq - 1], meta.at[0:n_seq - 1], meta_recv).wait()
    finish(x)
    do_chunk(2 * Z - 1)
    finish(1 - x)

    def share(i, carry):
        d = lax.rem(me + i, n_dev)
        pltpu.make_async_remote_copy(
            src_ref=part.at[me], dst_ref=part.at[me], send_sem=part_send, recv_sem=part_recv,
            device_id=(d // n_seq, d % n_seq), device_id_type=MESH,
        ).start()
        return carry

    lax.fori_loop(1, n_dev, share, 0)

    def sent(sem):
        pltpu.make_async_copy(G.at[0], G.at[0], sem).wait()

    def drain(zz, carry):
        for side in range(2):
            also = True if side == 0 else by_z(zz)

            @pl.when(jnp.logical_and(also, jnp.logical_and(zz <= z, z + 1 < Z)))
            def _():
                sent(up_sem.at[side, zz])

            @pl.when(jnp.logical_and(also, jnp.logical_and(zz >= z, z > 0)))
            def _():
                sent(down_sem.at[side, zz])

        @pl.when(jnp.logical_or(zz == z, jnp.logical_not(by_z(zz))))
        def _():
            sent(p_sem.at[zz])

        return carry

    lax.fori_loop(0, Z, drain, 0)
    for sem, count in ((q_sem, 2 * Z), (sib_sem, 4 * Z)):
        pltpu.make_async_copy(G.at[0:count], G.at[0:count], sem).wait()
    pltpu.make_async_copy(meta.at[0:n_seq - 1], meta.at[0:n_seq - 1], meta_send).wait()
    pltpu.make_async_copy(part.at[0:n_dev - 1], part.at[0:n_dev - 1], part_recv).wait()

    parts = part[...]
    lses, t = parts[:, :n_seq, :], jnp.sum(parts[:, n_seq:2 * n_seq, :], axis=0)
    top = jnp.max(lses, axis=0)
    lse = top + jnp.log(jnp.sum(jnp.exp(lses - top[None]), axis=0))
    keep = jnp.concatenate([meta[i, 1:2, :] for i in range(n_seq)], axis=0).astype(jnp.float32)
    loss = keep * (lse - t)

    def whole(a):
        return jnp.sum(jnp.sum(a, axis=0, keepdims=True), axis=1, keepdims=True)

    count = whole(keep)
    ce_ref[...] = whole(loss) / count
    zr_ref[...] = jnp.sqrt(whole(keep * lse * lse) / count)
    mine = lax.broadcasted_iota(jnp.int32, (n_seq, toks), 0) == s
    done[0:1, :] = jnp.sum(jnp.where(mine, lse, 0.0), axis=0, keepdims=True)
    done[1:2, :] = jnp.sum(jnp.where(mine, t, 0.0), axis=0, keepdims=True)
    out = pltpu.make_async_copy(done, tok_ref, in_sem.at[0])
    out.start()
    out.wait()
    pltpu.make_async_copy(part.at[0:n_dev - 1], part.at[0:n_dev - 1], part_send).wait()


def on_device(n_voc, n_seq, hidden, weight, targets, loss_mask):
    toks, feat = hidden.shape
    sub = 16
    voc, wide = weight.shape
    fits = (
        n_seq == 4 and n_voc % 2 == 0 and n_voc >= 8 and toks == LANES
        and feat % sub == 0 and 2 * feat % LANES == 0 and voc % 8 == 0
    )
    if not fits:
        return general(hidden, weight, targets, loss_mask)
    n_dev = n_voc * n_seq
    n_z = n_voc // 2
    f32 = jnp.float32
    dma = pltpu.SemaphoreType.DMA
    vmem = pl.BlockSpec(memory_space=pltpu.VMEM)
    hbm = pl.BlockSpec(memory_space=pltpu.HBM)
    tok, ce, root = pl.pallas_call(
        functools.partial(kernel, n_voc, n_seq),
        out_shape=(
            jax.ShapeDtypeStruct((2, toks), f32),
            jax.ShapeDtypeStruct((1, 1), f32),
            jax.ShapeDtypeStruct((1, 1), f32),
        ),
        in_specs=[hbm, hbm, hbm, hbm],
        out_specs=(hbm, vmem, vmem),
        scratch_shapes=[
            pltpu.VMEM((n_dev, feat, toks), jnp.bfloat16),
            pltpu.VMEM((voc, wide), jnp.bfloat16),
            pltpu.VMEM((2, voc, 2 * toks), f32),
            pltpu.VMEM((n_seq, 8, LANES), jnp.int32),
            pltpu.VMEM((n_dev, 2 * n_seq, LANES), f32),
            pltpu.VMEM((2, toks), f32),
            dma, dma((3,)), dma((n_dev,)), dma((2, n_z)), dma((2, n_z)),
            dma((n_z,)), dma, dma, dma, dma, dma, dma,
        ],
        compiler_params=pltpu.CompilerParams(
            collective_id=0, has_side_effects=True, vmem_limit_bytes=64 * 2**20
        ),
        cost_estimate=pl.CostEstimate(
            flops=2 * n_seq * toks * wide * voc, bytes_accessed=2 * voc * wide,
            transcendentals=n_seq * toks * voc,
        ),
    )(hidden.T, weight, targets.reshape(1, toks), loss_mask.reshape(1, toks))
    lse = tok[0]
    loss = loss_mask.astype(f32) * (lse - tok[1])
    return (lse, loss, ce.reshape(()), root.reshape(()))


def solution(mesh):
    in_specs = (P("seq", "vocab"), P(("vocab", "seq"), None), P("seq"), P("seq"))
    out_specs = (P("seq"), P("seq"), P(), P())
    return jax.shard_map(
        functools.partial(on_device, mesh.shape["vocab"], mesh.shape["seq"]),
        mesh=mesh, in_specs=in_specs, out_specs=out_specs, check_vma=False,
    )
```

```python
import functools
import jax
import jax.numpy as jnp
from jax import lax
from jax.experimental import pallas as pl
from jax.experimental.pallas import tpu as pltpu
from jax.sharding import PartitionSpec as P

MESH = pl.DeviceIdType.MESH
LANES = 128


def general(hidden, weight, targets, loss_mask):
    voc_local = weight.shape[0]
    all_ids = lax.all_gather(targets, "seq", axis=0, tiled=True)
    hidden = lax.all_gather(hidden, "vocab", axis=1, tiled=True)
    logits = lax.dot_general(
        lax.all_gather(hidden, "seq", axis=0, tiled=True),
        weight,
        (((1,), (1,)), ((), ())),
        preferred_element_type=jnp.float32,
    )
    block_index = lax.axis_index("vocab") * lax.axis_size("seq") + lax.axis_index("seq")
    columns = block_index * voc_local + jnp.arange(voc_local, dtype=jnp.int32)
    target_hit = columns[None, :] == all_ids[:, None]
    target_part = jnp.sum(jnp.where(target_hit, logits, jnp.float32(0.0)), axis=1)
    row_peak = lax.pmax(jnp.max(logits, axis=1), ("vocab", "seq"))
    exp_part = jnp.sum(jnp.exp(logits - row_peak[:, None]), axis=1)
    share_exp, share_target = (
        lax.psum_scatter(exp_part, "seq", scatter_dimension=0, tiled=True),
        lax.psum_scatter(target_part, "seq", scatter_dimension=0, tiled=True),
    )
    exp_total, target_logit = lax.psum((share_exp, share_target), "vocab")
    tok_local = targets.shape[0]
    own_peak = lax.dynamic_slice_in_dim(row_peak, lax.axis_index("seq") * tok_local, tok_local, 0)
    lse = own_peak + jnp.log(exp_total)
    keep = loss_mask.astype(jnp.float32)
    token_loss = keep * (lse - target_logit)
    loss_sum, square_sum, count = lax.psum(
        (jnp.sum(token_loss), jnp.sum(keep * lse * lse), jnp.sum(keep)), "seq"
    )
    return (lse, token_loss, loss_sum / count, jnp.sqrt(square_sum / count))


def kernel(
    n_voc, n_seq,
    h_ref, w_hbm, tgt_ref, msk_ref,
    tok_ref, ce_ref, zr_ref,
    G, W, acc, meta, part, done,
    w_sem, in_sem, recv, up_sem, down_sem, p_sem, q_sem, sib_sem, meta_send, meta_recv, part_send, part_recv,
):
    Z = n_voc // 2
    n_dev = n_voc * n_seq
    v, s = lax.axis_index("vocab"), lax.axis_index("seq")
    z, y, x, c = v // 2, v % 2, s // 2, s % 2
    me = v * n_seq + s
    voc = w_hbm.shape[0]
    feat, toks = h_ref.shape

    own = (
        pltpu.make_async_copy(h_ref, G.at[me], in_sem.at[0]),
        pltpu.make_async_copy(tgt_ref, meta.at[s, pl.ds(0, 1)], in_sem.at[1]),
        pltpu.make_async_copy(msk_ref, meta.at[s, pl.ds(1, 1)], in_sem.at[2]),
    )
    for copy in own:
        copy.start()
    load = pltpu.make_async_copy(w_hbm, W, w_sem)
    load.start()

    barrier = pltpu.get_barrier_semaphore()

    def greet(i, carry):
        d = lax.rem(me + i, n_dev)
        pl.semaphore_signal(barrier, inc=1, device_id=(d // n_seq, d % n_seq), device_id_type=MESH)
        return carry

    lax.fori_loop(1, n_dev, greet, 0)

    for copy in own:
        copy.wait()
    pl.semaphore_wait(barrier, n_dev - 1)

    flip_y, flip_x = 1 - 2 * y, 2 - 4 * x
    sib = s + 1 - 2 * c
    p_v, p_s = v + (1 - c) * flip_y, s + c * flip_x
    q_v, q_s = v + c * flip_y, s + (1 - c) * flip_x

    def block(zz, yy, ss):
        return (2 * zz + yy) * n_seq + ss

    def push(b, sem, dv, ds):
        pltpu.make_async_remote_copy(
            src_ref=G.at[b], dst_ref=G.at[b], send_sem=sem, recv_sem=recv.at[b],
            device_id=(dv, ds), device_id_type=MESH,
        ).start()

    def arrived(b):
        pltpu.make_async_remote_copy(
            src_ref=G.at[b], dst_ref=G.at[b], send_sem=sib_sem, recv_sem=recv.at[b],
            device_id=(v, sib), device_id_type=MESH,
        ).wait_recv()

    near = jnp.minimum(z, Z - 1 - z)
    far_side = jnp.where(2 * z < Z, 1, -1)

    def order(i):
        in_near = i <= 2 * near
        sgn = jnp.where(in_near, jnp.where(i % 2 == 1, -1, 1), far_side)
        dist = jnp.where(in_near, (i + 1) // 2, i - near)
        return z + sgn * dist

    def to_sib(b):
        push(b, sib_sem, v, sib)

    def along(b, zz):
        @pl.when(jnp.logical_and(zz <= z, z + 1 < Z))
        def _():
            push(b, up_sem.at[zz], v + 2, s)

        @pl.when(jnp.logical_and(zz >= z, z > 0))
        def _():
            push(b, down_sem.at[zz], v - 2, s)

    def line(zz):
        b = block(zz, y, s)
        along(b, zz)
        push(b, p_sem.at[zz], p_v, p_s)
        push(b, q_sem, q_v, q_s)
        to_sib(b)

    line(z)

    def tell(i, carry):
        d = lax.rem(s + i, n_seq)
        pltpu.make_async_remote_copy(
            src_ref=meta.at[s], dst_ref=meta.at[s], send_sem=meta_send, recv_sem=meta_recv,
            device_id=(v, d), device_id_type=MESH,
        ).start()
        return carry

    lax.fori_loop(1, n_seq, tell, 0)

    p_y, q_y = p_v % 2, q_v % 2

    def from_p(zz):
        b = block(zz, p_y, p_s)
        arrived(b)
        push(b, q_sem, q_v, q_s)
        to_sib(b)

    def from_q(zz, yy, ss):
        b = block(zz, yy, ss)
        arrived(b)
        to_sib(b)

    def chunk(zz, xx, first):
        sides = []
        for cc in range(2):
            pair = [G[block(zz, yy, 2 * xx + cc)] for yy in range(2)]
            sides.append(jnp.concatenate(pair, axis=0))
        rows = jnp.concatenate(sides, axis=1)
        cols = pl.ds(pl.multiple_of(zz * 2 * feat, LANES), 2 * feat)
        out = lax.dot_general(
            W[:, cols], rows, (((1,), (0,)), ((), ())), preferred_element_type=jnp.float32
        )

        @pl.when(first)
        def _():
            acc[xx] = out

        @pl.when(jnp.logical_not(first))
        def _():
            acc[xx] += out

    step = max(r for r in range(8, 257, 8) if voc % r == 0)

    def finish(xx):
        ids = jnp.concatenate([meta[2 * xx, 0:1, :], meta[2 * xx + 1, 0:1, :]], axis=1)
        ids = ids - me * voc
        wide = (8, 2 * toks)

        def peak(r, m):
            tile = acc[xx, pl.ds(pl.multiple_of(r * step, 8), step), :]
            return jnp.maximum(m, jnp.max(tile.reshape(step // 8, 8, 2 * toks), axis=0))

        m = lax.fori_loop(0, voc // step, peak, jnp.full(wide, -jnp.inf, jnp.float32))
        m = jnp.max(m, axis=0, keepdims=True)

        def total(r, carry):
            e, t = carry
            tile = acc[xx, pl.ds(pl.multiple_of(r * step, 8), step), :]
            row = lax.broadcasted_iota(jnp.int32, (step, 2 * toks), 0) + r * step
            hit = jnp.where(row == ids, tile, jnp.float32(0.0))
            e += jnp.sum(jnp.exp(tile - m).reshape(step // 8, 8, 2 * toks), axis=0)
            t += jnp.sum(hit.reshape(step // 8, 8, 2 * toks), axis=0)
            return e, t

        zero = jnp.zeros(wide, jnp.float32)
        e, t = lax.fori_loop(0, voc // step, total, (zero, zero))
        lse = m + jnp.log(jnp.sum(e, axis=0, keepdims=True))
        t = jnp.sum(t, axis=0, keepdims=True)
        for cc in range(2):
            cut = slice(cc * toks, (cc + 1) * toks)
            part[me, pl.ds(2 * xx + cc, 1), :] = lse[:, cut]
            part[me, pl.ds(n_seq + 2 * xx + cc, 1), :] = t[:, cut]

    def do_chunk(k):
        zz, far = order(k % Z), k // Z
        xx = x + far * (1 - 2 * x)
        ss = 2 * xx + 1 - c
        arrived(block(zz, 0, ss))
        arrived(block(zz, 1, ss))
        chunk(zz, xx, k % Z == 0)

    def turn(r, carry):
        @pl.when(r < Z)
        def _():
            zz = order(r)
            arrived(block(zz, y, s))
            line(zz)

        @pl.when(r <= Z)
        def _():
            from_p(order(r - 1))

        @pl.when(jnp.logical_and(r >= 2, r < Z + 2))
        def _():
            from_q(order(r - 2), q_y, q_s)

        @pl.when(r == 3)
        def _():
            load.wait()

        @pl.when(r >= 3)
        def _():
            from_q(order(r - 3), 1 - y, s + flip_x)
            do_chunk(r - 3)

        @pl.when(r >= 4)
        def _():
            do_chunk(Z + r - 4)

        return carry

    lax.fori_loop(1, Z + 3, turn, 0)
    pltpu.make_async_copy(meta.at[0:n_seq - 1], meta.at[0:n_seq - 1], meta_recv).wait()
    finish(x)
    do_chunk(2 * Z - 1)
    finish(1 - x)

    def share(i, carry):
        d = lax.rem(me + i, n_dev)
        pltpu.make_async_remote_copy(
            src_ref=part.at[me], dst_ref=part.at[me], send_sem=part_send, recv_sem=part_recv,
            device_id=(d // n_seq, d % n_seq), device_id_type=MESH,
        ).start()
        return carry

    lax.fori_loop(1, n_dev, share, 0)

    def sent(sem):
        pltpu.make_async_copy(G.at[0], G.at[0], sem).wait()

    def drain(zz, carry):
        @pl.when(jnp.logical_and(zz <= z, z + 1 < Z))
        def _():
            sent(up_sem.at[zz])

        @pl.when(jnp.logical_and(zz >= z, z > 0))
        def _():
            sent(down_sem.at[zz])

        sent(p_sem.at[zz])
        return carry

    lax.fori_loop(0, Z, drain, 0)
    for sem, count in ((q_sem, 2 * Z), (sib_sem, 4 * Z)):
        pltpu.make_async_copy(G.at[0:count], G.at[0:count], sem).wait()
    pltpu.make_async_copy(meta.at[0:n_seq - 1], meta.at[0:n_seq - 1], meta_send).wait()
    pltpu.make_async_copy(part.at[0:n_dev - 1], part.at[0:n_dev - 1], part_recv).wait()

    parts = part[...]
    lses, t = parts[:, :n_seq, :], jnp.sum(parts[:, n_seq:2 * n_seq, :], axis=0)
    top = jnp.max(lses, axis=0)
    lse = top + jnp.log(jnp.sum(jnp.exp(lses - top[None]), axis=0))
    keep = jnp.concatenate([meta[i, 1:2, :] for i in range(n_seq)], axis=0).astype(jnp.float32)
    loss = keep * (lse - t)

    def whole(a):
        return jnp.sum(jnp.sum(a, axis=0, keepdims=True), axis=1, keepdims=True)

    count = whole(keep)
    ce_ref[...] = whole(loss) / count
    zr_ref[...] = jnp.sqrt(whole(keep * lse * lse) / count)
    mine = lax.broadcasted_iota(jnp.int32, (n_seq, toks), 0) == s
    done[0:1, :] = jnp.sum(jnp.where(mine, lse, 0.0), axis=0, keepdims=True)
    done[1:2, :] = jnp.sum(jnp.where(mine, t, 0.0), axis=0, keepdims=True)
    out = pltpu.make_async_copy(done, tok_ref, in_sem.at[0])
    out.start()
    out.wait()
    pltpu.make_async_copy(part.at[0:n_dev - 1], part.at[0:n_dev - 1], part_send).wait()


def on_device(n_voc, n_seq, hidden, weight, targets, loss_mask):
    toks, feat = hidden.shape
    sub = 16
    voc, wide = weight.shape
    fits = (
        n_seq == 4 and n_voc % 2 == 0 and n_voc >= 8 and toks == LANES
        and feat % sub == 0 and 2 * feat % LANES == 0 and voc % 8 == 0
    )
    if not fits:
        return general(hidden, weight, targets, loss_mask)
    n_dev = n_voc * n_seq
    n_z = n_voc // 2
    f32 = jnp.float32
    dma = pltpu.SemaphoreType.DMA
    vmem = pl.BlockSpec(memory_space=pltpu.VMEM)
    hbm = pl.BlockSpec(memory_space=pltpu.HBM)
    tok, ce, root = pl.pallas_call(
        functools.partial(kernel, n_voc, n_seq),
        out_shape=(
            jax.ShapeDtypeStruct((2, toks), f32),
            jax.ShapeDtypeStruct((1, 1), f32),
            jax.ShapeDtypeStruct((1, 1), f32),
        ),
        in_specs=[hbm, hbm, hbm, hbm],
        out_specs=(hbm, vmem, vmem),
        scratch_shapes=[
            pltpu.VMEM((n_dev, feat, toks), jnp.bfloat16),
            pltpu.VMEM((voc, wide), jnp.bfloat16),
            pltpu.VMEM((2, voc, 2 * toks), f32),
            pltpu.VMEM((n_seq, 8, LANES), jnp.int32),
            pltpu.VMEM((n_dev, 2 * n_seq, LANES), f32),
            pltpu.VMEM((2, toks), f32),
            dma, dma((3,)), dma((n_dev,)), dma((n_z,)), dma((n_z,)),
            dma((n_z,)), dma, dma, dma, dma, dma, dma,
        ],
        compiler_params=pltpu.CompilerParams(
            collective_id=0, has_side_effects=True, vmem_limit_bytes=64 * 2**20
        ),
        cost_estimate=pl.CostEstimate(
            flops=2 * n_seq * toks * wide * voc, bytes_accessed=2 * voc * wide,
            transcendentals=n_seq * toks * voc,
        ),
    )(hidden.T, weight, targets.reshape(1, toks), loss_mask.reshape(1, toks))
    lse = tok[0]
    loss = loss_mask.astype(f32) * (lse - tok[1])
    return (lse, loss, ce.reshape(()), root.reshape(()))


def solution(mesh):
    in_specs = (P("seq", "vocab"), P(("vocab", "seq"), None), P("seq"), P("seq"))
    out_specs = (P("seq"), P("seq"), P(), P())
    return jax.shard_map(
        functools.partial(on_device, mesh.shape["vocab"], mesh.shape["seq"]),
        mesh=mesh, in_specs=in_specs, out_specs=out_specs, check_vma=False,
    )
```
